128 devices in a mesh: ctx: 64 (over y, z, x_lo, core), tp: 2 (over x_hi).
Axes of the slice: x: 4 (x_hi: 2, x_lo: 2; x = x_hi * 2 + x_lo), y: 4, z: 4, core: 2. Of those that a mesh axis runs over, the one named last changes fastest.
Arguments:
- ctx_query: bfloat16 [49152, 8192], P('ctx', 'tp'), may hold values from -27 to 27
- ctx_key: bfloat16 [49152, 1024], P('ctx', 'tp'), may hold values from -10.2 to 10.2
- ctx_value: bfloat16 [49152, 1024], P('ctx', 'tp'), may hold values from -6 to 6
- stretch_query: bfloat16 [256, 8192], P(('ctx', 'tp')), may hold values from -27 to 27
- stretch_key: bfloat16 [256, 1024], P('ctx', 'tp'), may hold values from -10.2 to 10.2
- stretch_value: bfloat16 [256, 1024], P('ctx', 'tp'), may hold values from -6 to 6
Outputs:
- context_out: bfloat16 [49152, 8192], P('ctx', 'tp')
- stretch_out: bfloat16 [256, 8192], P(('ctx', 'tp'))
The draws below stay inside these ranges and needn't reach their ends.
All inputs are finite; a program needn't handle non-finite values.
Results may differ from the reference program's by a relative error of at most 0.013.
Values may be sent and summed in bfloat16 or wider, within the bound.
A program may use at most 128 MiB of HBM per device.

```python
import jax
import jax.numpy as jnp
from jax import lax

HEADS = 64
KV_HEADS = 8
HEAD_DIM = 128
BLOCK = 768
ANCHOR = 384
CONTEXT = 49152
QLEN = 256
N_CTX = 64


def base_values(key, shape):
    return 1.7 * jnp.clip(jax.random.normal(key, shape, jnp.float32), -6.0, 6.0)


def draw_ctx_key(key, part):
    key = jax.random.fold_in(key, 21)
    result = base_values(key, (CONTEXT, KV_HEADS * HEAD_DIM))
    return result.astype(jnp.bfloat16)


def draw_ctx_query(key, part):
    key = jax.random.fold_in(key, 22)
    result = base_values(key, (CONTEXT, HEADS * HEAD_DIM))
    return result.astype(jnp.bfloat16)


def draw_stretch_key(key, part):
    key = jax.random.fold_in(key, 23)
    result = base_values(key, (QLEN, KV_HEADS * HEAD_DIM))
    return result.astype(jnp.bfloat16)


def draw_stretch_query(key, part):
    key = jax.random.fold_in(key, 24)
    result = base_values(key, (QLEN, HEADS * HEAD_DIM))
    return result.astype(jnp.bfloat16)


def shard_levels(key, extent, split, least, high):
    factor_of, own = 1.0, jax.random.fold_in(key, 6)
    for position, shards_of in split:
        heights = jnp.exp(jax.random.uniform(jax.random.fold_in(own, position), (shards_of,), jnp.float32, least / len(split), high / len(split)))
        factor_of = factor_of * jnp.repeat(heights, extent[position] // shards_of).reshape([-1 if axis == position else 1 for axis in range(len(extent))])
    return factor_of


def normal_values(rng, dims, scale, reach, split=(), held_as=jnp.bfloat16):
    entries = jax.random.normal(rng, dims, jnp.float32) * scale
    if len(split) > 0:
        entries = shard_levels(rng, dims, split, -0.22, 0.18) * entries
    return jnp.clip(entries, min=-reach, max=reach).astype(held_as)


def setup_inputs(seed: int = 0) -> dict:
    splits = jax.random.split(jax.random.key(seed), 7)
    return {
        "ctx_query": draw_ctx_query(jax.random.fold_in(splits[6], 71), 0),
        "ctx_key": draw_ctx_key(jax.random.fold_in(splits[6], 71), 0),
        "ctx_value": normal_values(splits[2], (CONTEXT, KV_HEADS * HEAD_DIM), 1.0, 6.0, ((0, 64), (1, 2))),
        "stretch_query": draw_stretch_query(jax.random.fold_in(splits[6], 71), 0),
        "stretch_key": draw_stretch_key(jax.random.fold_in(splits[6], 71), 0),
        "stretch_value": normal_values(splits[5], (QLEN, KV_HEADS * HEAD_DIM), 1.0, 6.0, ((0, 64), (1, 2))),
    }


def round_weights(probs):
    return lax.optimization_barrier(probs.astype(jnp.bfloat16)).astype(jnp.float32)


def context_part(ctx_query, ctx_key, ctx_value):
    group = HEADS // KV_HEADS
    scale = HEAD_DIM ** -0.5
    anchor_key = ctx_key[:ANCHOR]
    anchor_value = ctx_value[:ANCHOR]
    line = jnp.arange(BLOCK, dtype=jnp.int32)[:, None]
    column = jnp.arange(ANCHOR + BLOCK, dtype=jnp.int32)[None, :]

    def one_block(block):
        start = (block * BLOCK).astype(jnp.int32)
        queries = lax.dynamic_slice_in_dim(ctx_query, start, BLOCK, 0).astype(jnp.float32)
        queries = queries.reshape(BLOCK, KV_HEADS, group, HEAD_DIM)
        keys = jnp.concatenate([anchor_key, lax.dynamic_slice_in_dim(ctx_key, start, BLOCK, 0)], 0)
        values = jnp.concatenate([anchor_value, lax.dynamic_slice_in_dim(ctx_value, start, BLOCK, 0)], 0)
        keys = keys.astype(jnp.float32).reshape(ANCHOR + BLOCK, KV_HEADS, HEAD_DIM)
        values = values.astype(jnp.float32).reshape(ANCHOR + BLOCK, KV_HEADS, HEAD_DIM)
        scores = jnp.einsum("bgjd,kgd->gjbk", queries, keys, precision=lax.Precision.HIGHEST) * scale
        visible = jnp.where(column >= ANCHOR, column - ANCHOR <= line, block > 0)
        scores = jnp.where(visible, scores, -jnp.inf)
        probs = jnp.exp(scores - jnp.max(scores, axis=-1, keepdims=True))
        total = jnp.sum(probs, axis=-1)
        summed = jnp.einsum("gjbk,kgd->gjbd", round_weights(probs), values, precision=lax.Precision.HIGHEST)
        result = summed / total[..., None]
        return result.transpose(2, 0, 1, 3).reshape(BLOCK, HEADS * HEAD_DIM).astype(jnp.bfloat16)

    blocks = lax.map(one_block, jnp.arange(N_CTX, dtype=jnp.int32))
    return blocks.reshape(CONTEXT, HEADS * HEAD_DIM)


def stretch_part(stretch_query, stretch_key, stretch_value, ctx_key, ctx_value):
    group = HEADS // KV_HEADS
    scale = HEAD_DIM ** -0.5
    queries = stretch_query.astype(jnp.float32).reshape(QLEN, KV_HEADS, group, HEAD_DIM)

    def absorb(carry, keys, values, visible):
        peak, summed, total = carry
        keys = keys.astype(jnp.float32).reshape(-1, KV_HEADS, HEAD_DIM)
        values = values.astype(jnp.float32).reshape(-1, KV_HEADS, HEAD_DIM)
        scores = jnp.einsum("qgjd,kgd->gjqk", queries, keys, precision=lax.Precision.HIGHEST) * scale
        scores = jnp.where(visible, scores, -jnp.inf)
        new_peak = jnp.maximum(peak, jnp.max(scores, axis=-1))
        probs = jnp.exp(scores - new_peak[..., None])
        shrink = jnp.exp(peak - new_peak)
        summed = summed * shrink[..., None] + jnp.einsum("gjqk,kgd->gjqd", round_weights(probs), values, precision=lax.Precision.HIGHEST)
        total = total * shrink + jnp.sum(probs, axis=-1)
        return new_peak, summed, total

    start = (jnp.full((KV_HEADS, group, QLEN), -jnp.inf, jnp.float32),
             jnp.zeros((KV_HEADS, group, QLEN, HEAD_DIM), jnp.float32),
             jnp.zeros((KV_HEADS, group, QLEN), jnp.float32))

    def step(carry, pair):
        return absorb(carry, pair[0], pair[1], True), None

    key_blocks = ctx_key.reshape(N_CTX, BLOCK, KV_HEADS * HEAD_DIM)
    value_blocks = ctx_value.reshape(N_CTX, BLOCK, KV_HEADS * HEAD_DIM)
    carry, unused = lax.scan(step, start, (key_blocks, value_blocks))
    causal = jnp.arange(QLEN, dtype=jnp.int32)[None, :] <= jnp.arange(QLEN, dtype=jnp.int32)[:, None]
    peak, summed, total = absorb(carry, stretch_key, stretch_value, causal)
    result = summed / total[..., None]
    return result.transpose(2, 0, 1, 3).reshape(QLEN, HEADS * HEAD_DIM).astype(jnp.bfloat16)


def reference(ctx_query, ctx_key, ctx_value, stretch_query, stretch_key, stretch_value):
    context_out = context_part(ctx_query, ctx_key, ctx_value)
    stretch_out = stretch_part(stretch_query, stretch_key, stretch_value, ctx_key, ctx_value)
    return context_out, stretch_out
```

```python
import functools

import jax
import jax.numpy as jnp
from jax import lax
from jax.experimental import pallas as pl
from jax.experimental.pallas import tpu as pltpu
from jax.sharding import PartitionSpec as P

MESH = pl.DeviceIdType.MESH
D = 128
ANCHOR = 384
ROWS = 768
KEYS = ANCHOR + ROWS
GROUPS = 4
CHIPS = 32
LOG2E = 1.4426950408889634
C = D**-0.5 * LOG2E
NEG = -1e30
TILE = 128
TILES = ROWS // TILE
HS = 4
M = HS * TILE
HALVES = 8
TWO = 4
FIRST = 4
PIECE = 96
BF = jnp.bfloat16
F32 = jnp.float32


def scores_of(q, k):
    return lax.dot_general(q, k, (((1,), (1,)), ((), ())), preferred_element_type=F32)


def stacked(ref, i, t):
    rows = slice(t * TILE, (t + 1) * TILE)
    return jnp.concatenate([ref[i, rows, j * D : (j + 1) * D] for j in range(HS)], 0)


def unstack(ref, i, t, value):
    for j in range(HS):
        ref[i, t * TILE : (t + 1) * TILE, j * D : (j + 1) * D] = value[j * TILE : (j + 1) * TILE]


def mask_last(s):
    line = lax.broadcasted_iota(jnp.int32, (TILE, TILE), 0)
    column = lax.broadcasted_iota(jnp.int32, (TILE, TILE), 1)
    seen = column <= line
    n = s.shape[1]
    last = jnp.concatenate(
        [jnp.where(seen, s[j * TILE : (j + 1) * TILE, n - TILE :], NEG) for j in range(HS)], 0
    )
    return last if n == TILE else jnp.concatenate([s[:, : n - TILE], last], 1)


def in_order(items, first, second):
    s = first(items[0])
    for at, item in enumerate(items):
        later = first(items[at + 1]) if at + 1 < len(items) else None
        second(item, s)
        s = later


def own_step(i, qv, kcat, vcat, part):
    g = i // 2

    def first(t):
        n = TILE * (t + 1)
        return scores_of(stacked(qv, i, t), kcat[g, ANCHOR : ANCHOR + n, :])

    def second(t, s):
        n = TILE * (t + 1)
        s = mask_last(s)
        m = jnp.max(s, -1, keepdims=True)
        p = jnp.exp2((s - m) * C).astype(BF)
        o = jnp.dot(p, vcat[g, ANCHOR : ANCHOR + n, :], preferred_element_type=F32)
        total = o[:, D:]
        part[i, t, :, :D] = o[:, :D] / total
        part[i, t, :, D:] = m + jnp.log(total) * (LOG2E / C)

    in_order(list(range(TILES)), first, second)


def anchor_step(i, qv, kcat, vcat, part, ov):
    g = i // 2

    def first(t):
        return scores_of(stacked(qv, i, t), kcat[g, :ANCHOR, :])

    def second(t, s):
        held = part[i, t, :, D:]
        m = jnp.maximum(jnp.max(s, -1, keepdims=True), held)
        p = [jnp.exp2((s[:, j * D : (j + 1) * D] - m) * C).astype(BF) for j in range(ANCHOR // D)]
        o = jnp.dot(jnp.concatenate(p, 1), vcat[g, :ANCHOR, :], preferred_element_type=F32)
        e = jnp.exp2((held - m) * C)
        unstack(ov, i, t, ((o[:, :D] + e * part[i, t, :, :D]) / (o[:, D:] + e)).astype(BF))

    in_order(list(range(TILES)), first, second)


def whole_step(q_ref, i, o_ref, o_at, kcat, vcat, g):
    def first(t):
        return scores_of(stacked(q_ref, i, t), kcat[g, : ANCHOR + TILE * (t + 1), :])

    def second(t, s):
        s = mask_last(s)
        m = jnp.max(s, -1, keepdims=True)
        p = jnp.exp2((s - m) * C).astype(BF)
        o = jnp.dot(p, vcat[g, : ANCHOR + TILE * (t + 1), :], preferred_element_type=F32)
        unstack(o_ref, o_at, t, (o[:, :D] / o[:, D:]).astype(BF))

    in_order(list(range(TILES)), first, second)


def stretch_step(gl, core, got, kcat, vcat, kpeer, vpeer, sent, lse):
    g = core * 2 + gl
    near = 8
    size = near * 64
    line = lax.broadcasted_iota(jnp.int32, (64, D), 0)
    column = lax.broadcasted_iota(jnp.int32, (64, D), 1)
    mine = column == line + 64 * gl

    def first(at):
        q = got[at * near : (at + 1) * near, 0:4, gl].reshape(size, D)
        return scores_of(q, kcat[g, ANCHOR:, :]), scores_of(q, kpeer[gl])

    def second(at, s):
        own, peer = s
        m = jnp.maximum(jnp.max(own, -1, keepdims=True), jnp.max(peer, -1, keepdims=True))
        own = jnp.exp2((own - m) * C).astype(BF)
        peer = jnp.exp2((peer - m) * C).astype(BF)
        o = jnp.dot(own, vcat[g, ANCHOR:, :], preferred_element_type=F32) + jnp.dot(
            peer, vpeer[gl], preferred_element_type=F32
        )
        total = o[:, D:]
        value = (o[:, :D] / total).astype(BF).reshape(near, 4, 16, D)
        sent[at * near : (at + 1) * near, pl.ds(gl * 4, 4)] = value
        level = m * C + jnp.log(total) * LOG2E
        level = jnp.where(mine[None], level.reshape(near, 64, D), 0.0)
        lse[gl, at * near : (at + 1) * near, :] = jnp.sum(level, axis=1)

    in_order(list(range(CHIPS // near)), first, second)


def level_tile(level):
    high = level.astype(BF).astype(F32)
    middle = (level - high).astype(BF).astype(F32)
    low = level - high - middle
    row = lax.broadcasted_iota(jnp.int32, (16, D), 0)
    tile = jnp.where(row == 0, high, jnp.where(row == 1, middle, jnp.where(row == 2, low, 0.0)))
    return tile.astype(BF)


def self_step(chip, got, parts):
    plain = got[:, 4].reshape(1024, D)
    held = plain.astype(F32)
    moved = jnp.concatenate([held[1016:], held[:1016]], 0).astype(BF)
    place = lax.broadcasted_iota(jnp.int32, (64, 1024), 1)
    line = chip * 8 + lax.broadcasted_iota(jnp.int32, (64, 1024), 0) // 8
    key = (place // 16) * 4 + place % 4
    here = lax.broadcasted_iota(jnp.int32, (64, D), 0)
    column = lax.broadcasted_iota(jnp.int32, (64, D), 1)
    level = jnp.zeros((1, D), F32)
    for gl in range(2):
        q = got[chip, 0:4, gl].reshape(64, D)
        s = scores_of(q, moved)
        s = jnp.where((key <= line) & ((place // 4) % 4 == 2 + gl), s, NEG)
        m = jnp.max(s, -1, keepdims=True)
        p = jnp.exp2((s - m) * C)
        total = jnp.sum(p, -1, keepdims=True)
        o = jnp.dot(p.astype(BF), plain, preferred_element_type=F32) / total
        parts[CHIPS, gl * 4 : (gl + 1) * 4] = o.astype(BF).reshape(4, 16, D)
        mine = jnp.where(column == here + 64 * gl, m * C + jnp.log(total) * LOG2E, 0.0)
        level = level + jnp.sum(mine, axis=0, keepdims=True)
    parts[CHIPS, 8] = level_tile(level)


def merge_step(parts, wide):
    def level_of(s):
        tile = parts[s, 8].astype(F32)
        return tile[0:1] + tile[1:2] + tile[2:3]

    levels = [level_of(s) for s in range(CHIPS + 1)]
    top = functools.reduce(jnp.maximum, levels)
    weights = [jnp.exp2(level - top) for level in levels]
    total = functools.reduce(jnp.add, weights)
    line = lax.broadcasted_iota(jnp.int32, (D, D), 0)
    column = lax.broadcasted_iota(jnp.int32, (D, D), 1)
    same = line == column
    for s in range(CHIPS + 1):
        wide[s, 0:1] = weights[s] / total

    def add(s, result):
        factor = jnp.sum(jnp.where(same, wide[s, 0:1], 0.0), -1, keepdims=True)
        return result + factor * parts[s, 0:8].astype(F32).reshape(D, D)

    return lax.fori_loop(0, CHIPS + 1, add, jnp.zeros((D, D), F32))


def first_kernel(
    cq, ck, cv, sq, sk, sv,
    out, anchor_key, anchor_value, stretch_out,
    qv, kcat, vcat, kpeer, vpeer, cls, clskv, got, anc, part, ov, sent, parts, lse, wide, mine, last,
    kvtiles,
    load_q, load_k, load_v, load_a, put,
    send0, recv0, recv0kv, swap_send, swap_recv, send1, recv1,
    scatter_send, scatter_recv, anc_send, anc_recv, core_send, core_recv,
    send2, recv2, send3, recv3,
):
    ctx, tp = lax.axis_index("ctx"), lax.axis_index("tp")
    chip, core = ctx // 2, ctx % 2
    me = core * 2 + tp

    def at_chip(other):
        return (other * 2 + core, tp)

    def at_class(other):
        return (chip * 2 + other // 2, other % 2)

    def remote(src, dst, send, recv, device):
        return pltpu.make_async_remote_copy(
            src_ref=src, dst_ref=dst, send_sem=send, recv_sem=recv, device_id=device, device_id_type=MESH
        )

    def wait_for(ref, sem):
        pltpu.make_async_copy(ref, ref, sem).wait()

    peer = (chip * 2 + 1 - core, tp)

    for g in range(GROUPS):
        columns = slice(g * D, (g + 1) * D)
        pltpu.make_async_copy(ck.at[:, columns], kcat.at[g, pl.ds(ANCHOR, ROWS)], load_k.at[g]).start()
        pltpu.make_async_copy(
            cv.at[:, columns], vcat.at[g, pl.ds(ANCHOR, ROWS), pl.ds(0, D)], load_v.at[g]
        ).start()
    for i in range(FIRST):
        pltpu.make_async_copy(cq.at[:, i * HS * D : (i + 1) * HS * D], qv.at[i], load_q.at[i]).start()

    @pl.when(ctx == 0)
    def _():
        for b in range(8):
            source = (ck if b < 4 else cv).at[:ANCHOR, (b % 4) * D : (b % 4 + 1) * D]
            pltpu.make_async_copy(source, anc.at[b * ANCHOR : (b + 1) * ANCHOR], load_a.at[b]).start()

    barrier = pltpu.get_barrier_semaphore()

    def greet(k, carry):
        pl.semaphore_signal(barrier, inc=1, device_id=at_chip((chip + k) % CHIPS), device_id_type=MESH)
        return carry

    lax.fori_loop(1, CHIPS, greet, 0)
    for k in range(1, 4):
        pl.semaphore_signal(barrier, inc=1, device_id=at_class((me + k) % 4), device_id_type=MESH)

    held = sq[...].astype(F32)
    for other in range(4):
        for gl in range(2):
            head = (other % 2) * 32 + (other // 2) * 16 + gl * 8
            rows = [held[r : r + 1, (head + h) * D : (head + h + 1) * D] for r in range(2) for h in range(8)]
            cls[other, gl] = jnp.concatenate(rows, 0).astype(BF)
    for b, ref in enumerate((sk, sv)):
        held = ref[...].astype(F32)
        for other in range(2):
            for gl in range(2):
                at = (other * 2 + gl) * D
                kvtiles[other, b * 8 + gl * 4 : b * 8 + gl * 4 + 4, :] = held[:, at : at + D]
    clskv[...] = kvtiles[...].astype(BF)
    got[chip, me] = cls[me]
    got[chip, 4, core] = clskv[core]

    pl.semaphore_wait(barrier, CHIPS - 1 + 3)

    for k in range(1, 4):
        other = (me + k) % 4
        remote(cls.at[other], got.at[chip, me], send0.at[0], recv0, at_class(other)).start()
    remote(clskv.at[1 - core], got.at[chip, 4, core], send0.at[1], recv0kv, peer).start()

    @pl.when(ctx == 0)
    def _():
        for b in range(8):
            rows = anc.at[b * ANCHOR : (b + 1) * ANCHOR]
            wait_for(rows, load_a.at[b])

        def scatter(other, carry):
            rows = anc.at[pl.ds(other * PIECE, PIECE)]
            remote(rows, rows, scatter_send, scatter_recv, at_chip(other)).start()
            return carry

        lax.fori_loop(1, CHIPS, scatter, 0)

    vcat[:, :, D:] = jnp.ones((GROUPS, KEYS, D), BF)
    vpeer[:, :, D:] = jnp.ones((2, ROWS, D), BF)

    wait_for(got.at[0, 0:3], recv0)
    wait_for(got.at[0, 4, 0], recv0kv)

    def spread(k, carry):
        rows = got.at[chip]
        remote(rows, rows, send1, recv1, at_chip((chip + k) % CHIPS)).start()
        return carry

    lax.fori_loop(1, CHIPS, spread, 0)

    for g in range(GROUPS):
        wait_for(kcat.at[g, pl.ds(ANCHOR, ROWS)], load_k.at[g])
        wait_for(vcat.at[g, pl.ds(ANCHOR, ROWS), pl.ds(0, D)], load_v.at[g])
    swaps = []
    for gl in range(2):
        g = (1 - core) * 2 + gl
        swaps.append(
            remote(
                kcat.at[g, pl.ds(ANCHOR, ROWS)], kpeer.at[gl], swap_send.at[gl], swap_recv.at[gl], peer
            )
        )
        swaps.append(
            remote(
                vcat.at[g, pl.ds(ANCHOR, ROWS), pl.ds(0, D)],
                vpeer.at[gl, :, pl.ds(0, D)],
                swap_send.at[2 + gl],
                swap_recv.at[2 + gl],
                peer,
            )
        )
    for copy in swaps:
        copy.start()

    piece = anc.at[pl.ds(chip * PIECE, PIECE)]

    def own(i, carry):
        wait_for(qv.at[i], load_q.at[i])
        own_step(i, qv, kcat, vcat, part)

        @pl.when((i == 0) & (core == 0))
        def _():
            @pl.when(chip != 0)
            def _():
                wait_for(piece, scatter_recv)

            def pass_on(k, carry):
                other = (chip + k) % CHIPS

                @pl.when(other != 0)
                def _():
                    remote(piece, piece, anc_send, anc_recv, at_chip(other)).start()

                return carry

            lax.fori_loop(1, CHIPS, pass_on, 0)

        return carry

    lax.fori_loop(0, TWO, own, 0)

    wait_for(got.at[0 : CHIPS - 1], recv1)
    for copy in swaps:
        copy.wait_recv()

    def stretch(gl, carry):
        stretch_step(gl, core, got, kcat, vcat, kpeer, vpeer, sent, lse)

        @pl.when((gl == 0) & (core == 0))
        def _():
            @pl.when(chip != 0)
            def _():
                wait_for(anc.at[: (CHIPS - 1) * PIECE], anc_recv)

            remote(anc, anc, core_send, core_recv, peer).start()

        return carry

    lax.fori_loop(0, 2, stretch, 0)
    for other in range(CHIPS):
        sent[other, 8] = level_tile(lse[0, other : other + 1, :] + lse[1, other : other + 1, :])

    def give(k, carry):
        other = (chip + k) % CHIPS
        remote(sent.at[other], parts.at[chip], send2, recv2, at_chip(other)).start()
        return carry

    lax.fori_loop(1, CHIPS, give, 0)
    parts[chip] = sent[chip]
    self_step(chip, got, parts)

    @pl.when(core == 1)
    def _():
        wait_for(anc, core_recv)

    for g in range(GROUPS):
        kcat[g, :ANCHOR, :] = anc[g * ANCHOR : (g + 1) * ANCHOR, :]
        vcat[g, :ANCHOR, :D] = anc[(GROUPS + g) * ANCHOR : (GROUPS + g + 1) * ANCHOR, :]

    @pl.when(ctx == 0)
    def _():
        for g in range(GROUPS):
            key = kcat[g, ANCHOR : ANCHOR + 16, :].astype(F32)[0:1]
            kcat[g, :ANCHOR, :] = jnp.broadcast_to(key, (ANCHOR, D)).astype(BF)
            vcat[g, :ANCHOR, :] = jnp.zeros((ANCHOR, 2 * D), BF)

    rest = FIRST // 2
    hand = [
        pltpu.make_async_copy(kcat.at[pl.ds(rest, GROUPS - rest), pl.ds(0, ANCHOR)], anchor_key, put.at[FIRST]),
        pltpu.make_async_copy(vcat.at[pl.ds(rest, GROUPS - rest), pl.ds(0, ANCHOR)], anchor_value, put.at[FIRST + 1]),
    ]
    for copy in hand:
        copy.start()

    def anchored(i, carry):
        anchor_step(i, qv, kcat, vcat, part, ov)
        pltpu.make_async_copy(ov.at[i], out.at[i], put.at[i]).start()
        return carry

    lax.fori_loop(0, TWO, anchored, 0)

    wait_for(parts.at[0 : CHIPS - 1], recv2)
    merged = merge_step(parts, wide).astype(BF).reshape(2, 4, 16, D)
    for gl in range(2):
        mine[:, gl] = merged[gl]
    for k in range(1, 4):
        other = (me + k) % 4
        remote(mine.at[other], last.at[me], send3, recv3, at_class(other)).start()
    last[me] = mine[me]
    wait_for(last.at[0:3], recv3)
    stretch_out[...] = last[...]

    for i in range(FIRST):
        pltpu.make_async_copy(ov.at[i], out.at[i], put.at[i]).wait()
    for copy in hand:
        copy.wait()
    wait_for(cls.at[0:3], send0.at[0])
    wait_for(clskv.at[0], send0.at[1])
    for copy in swaps:
        copy.wait_send()
    wait_for(got.at[0 : CHIPS - 1], send1)
    wait_for(sent.at[0 : CHIPS - 1], send2)
    wait_for(mine.at[0:3], send3)

    @pl.when(ctx == 0)
    def _():
        wait_for(anc.at[: (CHIPS - 1) * PIECE], scatter_send)

    @pl.when(core == 0)
    def _():
        wait_for(anc, core_send)

        @pl.when(chip == 0)
        def _():
            wait_for(anc.at[: (CHIPS - 1) * PIECE], anc_send)

        @pl.when(chip != 0)
        def _():
            wait_for(anc.at[: (CHIPS - 2) * PIECE], anc_send)


def first_call(cq, ck, cv, sq, sk, sv):
    dma = pltpu.SemaphoreType.DMA
    vmem = pltpu.VMEM
    anywhere = pl.BlockSpec(memory_space=pl.ANY)
    near = pl.BlockSpec(memory_space=pltpu.VMEM)
    rest = GROUPS - FIRST // 2
    return pl.pallas_call(
        first_kernel,
        in_specs=[anywhere, anywhere, anywhere, near, near, near],
        out_specs=[anywhere, anywhere, anywhere, near],
        out_shape=[
            jax.ShapeDtypeStruct((FIRST, ROWS, HS * D), BF),
            jax.ShapeDtypeStruct((rest, ANCHOR, D), BF),
            jax.ShapeDtypeStruct((rest, ANCHOR, 2 * D), BF),
            jax.ShapeDtypeStruct((4, 2, 16, D), BF),
        ],
        scratch_shapes=[
            vmem((FIRST, ROWS, HS * D), BF),
            vmem((GROUPS, KEYS, D), BF),
            vmem((GROUPS, KEYS, 2 * D), BF),
            vmem((2, ROWS, D), BF),
            vmem((2, ROWS, 2 * D), BF),
            vmem((4, 2, 16, D), BF),
            vmem((2, 16, D), BF),
            vmem((CHIPS, 5, 2, 16, D), BF),
            vmem((8 * ANCHOR, D), BF),
            vmem((TWO, TILES, M, 2 * D), F32),
            vmem((FIRST, ROWS, HS * D), BF),
            vmem((CHIPS, 9, 16, D), BF),
            vmem((CHIPS + 1, 9, 16, D), BF),
            vmem((2, CHIPS, D), F32),
            vmem((CHIPS + 1, 8, D), F32),
            vmem((4, 2, 16, D), BF),
            vmem((4, 2, 16, D), BF),
            vmem((2, 16, D), F32),
            dma((FIRST,)), dma((GROUPS,)), dma((GROUPS,)), dma((8,)), dma((FIRST + 2,)),
            dma((2,)), dma, dma, dma((4,)), dma((4,)), dma, dma,
            dma, dma, dma, dma, dma, dma,
            dma, dma, dma, dma,
        ],
        compiler_params=pltpu.CompilerParams(
            collective_id=0, has_side_effects=True, vmem_limit_bytes=58 * 2**20
        ),
        name="gather_stretch_first_heads",
    )(cq, ck, cv, sq, sk, sv)


def second_kernel(q, k, v, ak, av, before, out, kcat, vcat, ov, passing, put, fetch, carry):
    i = pl.program_id(0)
    fetches = [pltpu.make_async_copy(before.at[j], passing.at[j], fetch.at[j]) for j in range(FIRST)]
    moves = [
        pltpu.make_async_copy(passing.at[j], out.at[:, j * HS * D : (j + 1) * HS * D], carry.at[j])
        for j in range(FIRST)
    ]

    @pl.when(i == 0)
    def _():
        for copy in fetches:
            copy.start()

    @pl.when(i == 1)
    def _():
        for come, go in zip(fetches, moves):
            come.wait()
            go.start()

    @pl.when(i % 2 == 0)
    def _():
        kcat[0, :ANCHOR, :] = ak[0]
        kcat[0, ANCHOR:, :] = k[...]
        vcat[0, :ANCHOR, :] = av[0]
        vcat[0, ANCHOR:, :D] = v[...]
        vcat[0, ANCHOR:, D:] = jnp.ones((ROWS, D), BF)

    def result(step):
        columns = pl.ds(pl.multiple_of((FIRST + step) * HS * D, HS * D), HS * D)
        return pltpu.make_async_copy(ov.at[step], out.at[:, columns], put.at[step])

    whole_step(q, 0, ov, i, kcat, vcat, 0)
    result(i).start()

    @pl.when(i == HALVES - FIRST - 1)
    def _():
        for step in range(HALVES - FIRST):
            result(step).wait()
        for copy in moves:
            copy.wait()


def second_call(cq, ck, cv, ak, av, before):
    steps = HALVES - FIRST
    base = FIRST // 2
    return pl.pallas_call(
        lambda q, *rest: second_kernel(OneStep(q), *rest),
        grid=(steps,),
        in_specs=[
            pl.BlockSpec((ROWS, HS * D), lambda i: (0, FIRST + i)),
            pl.BlockSpec((ROWS, D), lambda i: (0, base + i // 2)),
            pl.BlockSpec((ROWS, D), lambda i: (0, base + i // 2)),
            pl.BlockSpec((1, ANCHOR, D), lambda i: (i // 2, 0, 0)),
            pl.BlockSpec((1, ANCHOR, 2 * D), lambda i: (i // 2, 0, 0)),
            pl.BlockSpec(memory_space=pl.ANY),
        ],
        out_specs=pl.BlockSpec(memory_space=pl.ANY),
        out_shape=jax.ShapeDtypeStruct((ROWS, 2 * GROUPS * HS * D), BF),
        scratch_shapes=[
            pltpu.VMEM((1, KEYS, D), BF),
            pltpu.VMEM((1, KEYS, 2 * D), BF),
            pltpu.VMEM((steps, ROWS, HS * D), BF),
            pltpu.VMEM((FIRST, ROWS, HS * D), BF),
            pltpu.SemaphoreType.DMA((steps,)),
            pltpu.SemaphoreType.DMA((FIRST,)),
            pltpu.SemaphoreType.DMA((FIRST,)),
        ],
        compiler_params=pltpu.CompilerParams(vmem_limit_bytes=58 * 2**20),
        name="last_heads",
    )(cq, ck, cv, ak, av, before)


class OneStep:
    def __init__(self, ref):
        self.ref = ref

    def __getitem__(self, index):
        return self.ref[index[1:]]


def body(cq, ck, cv, sq, sk, sv):
    before, anchor_key, anchor_value, stretch_out = first_call(cq, ck, cv, sq, sk, sv)
    stretch_out = stretch_out.reshape(2, 2, 2, 2, 8, D).transpose(3, 1, 0, 2, 4, 5).reshape(2, 64 * D)
    return second_call(cq, ck, cv, anchor_key, anchor_value, before), stretch_out


def solution(mesh):
    in_specs = (
        P("ctx", "tp"),
        P("ctx", "tp"),
        P("ctx", "tp"),
        P(("ctx", "tp"), None),
        P("ctx", "tp"),
        P("ctx", "tp"),
    )
    out_specs = (P("ctx", "tp"), P(("ctx", "tp"), None))
    return jax.shard_map(body, mesh=mesh, in_specs=in_specs, out_specs=out_specs, check_vma=False)
```

```python
import functools

import jax
import jax.numpy as jnp
from jax import lax
from jax.experimental import pallas as pl
from jax.experimental.pallas import tpu as pltpu
from jax.sharding import PartitionSpec as P

MESH = pl.DeviceIdType.MESH
D = 128
ANCHOR = 384
ROWS = 768
KEYS = ANCHOR + ROWS
GROUPS = 4
CHIPS = 32
LOG2E = 1.4426950408889634
C = D**-0.5 * LOG2E
NEG = -1e30
TILE = 128
TILES = ROWS // TILE
DOWN = list(range(TILES))[::-1]
HS = 4
M = HS * TILE
HALVES = 8
FIRST = 7
EARLY = 6
MERGE = 5
PIECE = 96
BF = jnp.bfloat16
F32 = jnp.float32


def scores_of(q, k):
    return lax.dot_general(q, k, (((1,), (1,)), ((), ())), preferred_element_type=F32)


def stacked(ref, i, t):
    rows = slice(t * TILE, (t + 1) * TILE)
    return jnp.concatenate([ref[i, rows, j * D : (j + 1) * D] for j in range(HS)], 0)


def unstack(ref, i, t, value):
    for j in range(HS):
        ref[i, t * TILE : (t + 1) * TILE, j * D : (j + 1) * D] = value[j * TILE : (j + 1) * TILE]


def mask_last(s):
    line = lax.broadcasted_iota(jnp.int32, (TILE, TILE), 0)
    column = lax.broadcasted_iota(jnp.int32, (TILE, TILE), 1)
    seen = column <= line
    n = s.shape[1]
    last = jnp.concatenate(
        [jnp.where(seen, s[j * TILE : (j + 1) * TILE, n - TILE :], NEG) for j in range(HS)], 0
    )
    return last if n == TILE else jnp.concatenate([s[:, : n - TILE], last], 1)


def in_order(items, first, second, between=None):
    s = first(items[0])
    for at, item in enumerate(items):
        if between is not None and at == len(items) // 2:
            between()
        later = first(items[at + 1]) if at + 1 < len(items) else None
        second(item, s)
        s = later


def own_step(i, qv, kcat, vcat, part):
    g = i // 2

    def first(t):
        n = TILE * (t + 1)
        return scores_of(stacked(qv, i, t), kcat[g, ANCHOR : ANCHOR + n, :])

    def second(t, s):
        n = TILE * (t + 1)
        s = mask_last(s)
        m = jnp.max(s, -1, keepdims=True)
        p = jnp.exp2((s - m) * C).astype(BF)
        o = jnp.dot(p, vcat[g, ANCHOR : ANCHOR + n, :], preferred_element_type=F32)
        total = o[:, D:]
        part[i, t, :, :D] = o[:, :D] / total
        part[i, t, :, D:] = m + jnp.log(total) * (LOG2E / C)

    in_order(DOWN, first, second)


def anchor_step(i, qv, kcat, vcat, part, done):
    g = i // 2

    def first(t):
        return scores_of(stacked(qv, i, t), kcat[g, :ANCHOR, :])

    def second(t, s):
        held = part[i, t, :, D:]
        m = jnp.maximum(jnp.max(s, -1, keepdims=True), held)
        p = [jnp.exp2((s[:, j * D : (j + 1) * D] - m) * C).astype(BF) for j in range(ANCHOR // D)]
        o = jnp.dot(jnp.concatenate(p, 1), vcat[g, :ANCHOR, :], preferred_element_type=F32)
        e = jnp.exp2((held - m) * C)
        unstack(qv, i, t, ((o[:, :D] + e * part[i, t, :, :D]) / (o[:, D:] + e)).astype(BF))
        done(t)

    in_order(list(range(TILES)), first, second)


def whole_step(q_ref, i, o_ref, o_at, kcat, vcat, g, done, between):
    def first(t):
        return scores_of(stacked(q_ref, i, t), kcat[g, : ANCHOR + TILE * (t + 1), :])

    def second(t, s):
        s = mask_last(s)
        m = jnp.max(s, -1, keepdims=True)
        p = jnp.exp2((s - m) * C).astype(BF)
        o = jnp.dot(p, vcat[g, : ANCHOR + TILE * (t + 1), :], preferred_element_type=F32)
        unstack(o_ref, o_at, t, (o[:, :D] / o[:, D:]).astype(BF))
        done(t)

    in_order(DOWN, first, second, between)


def stretch_step(gl, core, got, kcat, vcat, kpeer, vpeer, sent, lse):
    g = core * 2 + gl
    near = 8
    size = near * 64
    line = lax.broadcasted_iota(jnp.int32, (64, D), 0)
    column = lax.broadcasted_iota(jnp.int32, (64, D), 1)
    mine = column == line + 64 * gl

    def first(at):
        q = got[gl, at * near : (at + 1) * near].reshape(size, D)
        return scores_of(q, kcat[g, ANCHOR:, :]), scores_of(q, kpeer[gl])

    def second(at, s):
        own, peer = s
        m = jnp.maximum(jnp.max(own, -1, keepdims=True), jnp.max(peer, -1, keepdims=True))
        own = jnp.exp2((own - m) * C).astype(BF)
        peer = jnp.exp2((peer - m) * C).astype(BF)
        o = jnp.dot(own, vcat[g, ANCHOR:, :], preferred_element_type=F32) + jnp.dot(
            peer, vpeer[gl], preferred_element_type=F32
        )
        total = o[:, D:]
        value = (o[:, :D] / total).astype(BF).reshape(near, 4, 16, D)
        sent[at * near : (at + 1) * near, pl.ds(gl * 4, 4)] = value
        level = m * C + jnp.log(total) * LOG2E
        level = jnp.where(mine[None], level.reshape(near, 64, D), 0.0)
        lse[gl, at * near : (at + 1) * near, :] = jnp.sum(level, axis=1)

    in_order(list(range(CHIPS // near)), first, second)


def level_tile(level):
    high = level.astype(BF).astype(F32)
    middle = (level - high).astype(BF).astype(F32)
    low = level - high - middle
    row = lax.broadcasted_iota(jnp.int32, (16, D), 0)
    tile = jnp.where(row == 0, high, jnp.where(row == 1, middle, jnp.where(row == 2, low, 0.0)))
    return tile.astype(BF)


def self_step(chip, got, gotkv, parts):
    plain = gotkv[...].reshape(1024, D)
    held = plain.astype(F32)
    moved = jnp.concatenate([held[1016:], held[:1016]], 0).astype(BF)
    place = lax.broadcasted_iota(jnp.int32, (64, 1024), 1)
    line = chip * 8 + lax.broadcasted_iota(jnp.int32, (64, 1024), 0) // 8
    key = (place // 16) * 4 + place % 4
    here = lax.broadcasted_iota(jnp.int32, (64, D), 0)
    column = lax.broadcasted_iota(jnp.int32, (64, D), 1)
    level = jnp.zeros((1, D), F32)
    for gl in range(2):
        q = got[gl, chip].reshape(64, D)
        s = scores_of(q, moved)
        s = jnp.where((key <= line) & ((place // 4) % 4 == 2 + gl), s, NEG)
        m = jnp.max(s, -1, keepdims=True)
        p = jnp.exp2((s - m) * C)
        total = jnp.sum(p, -1, keepdims=True)
        o = jnp.dot(p.astype(BF), plain, preferred_element_type=F32) / total
        parts[CHIPS, gl * 4 : (gl + 1) * 4] = o.astype(BF).reshape(4, 16, D)
        mine = jnp.where(column == here + 64 * gl, m * C + jnp.log(total) * LOG2E, 0.0)
        level = level + jnp.sum(mine, axis=0, keepdims=True)
    parts[CHIPS, 8] = level_tile(level)


def merge_step(parts):
    def level_of(s):
        tile = parts[s, 8].astype(F32)
        return tile[0:1] + tile[1:2] + tile[2:3]

    levels = [level_of(s) for s in range(CHIPS + 1)]
    top = functools.reduce(jnp.maximum, levels)
    weights = [jnp.exp2(level - top) for level in levels]
    total = functools.reduce(jnp.add, weights)
    line = lax.broadcasted_iota(jnp.int32, (D, D), 0)
    column = lax.broadcasted_iota(jnp.int32, (D, D), 1)
    same = line == column
    result = jnp.zeros((D, D), F32)
    for s in range(CHIPS + 1):
        factor = jnp.sum(jnp.where(same, weights[s] / total, 0.0), -1, keepdims=True)
        result = result + factor * parts[s, 0:8].astype(F32).reshape(D, D)
    return result


def first_kernel(
    cq, ck, cv, sq_in, sk_in, sv_in,
    out, keys_out, values_out, stretch_out,
    sq, sk, sv, qv, kcat, vcat, kpeer, vpeer, cls, clskv, got, gotkv, anc, part, sent, parts, lse, mine, last, kvtiles,
    load_s, load_q, load_k, load_v, load_a, put,
    send0, recv0, recv0kv, swap_send, swap_recv, send1, recv1, send1kv, recv1kv,
    scatter_send, scatter_recv, anc_send, anc_recv, core_send, core_recv,
    send2, recv2, send3, recv3,
):
    ctx, tp = lax.axis_index("ctx"), lax.axis_index("tp")
    chip, core = ctx // 2, ctx % 2
    me = core * 2 + tp

    def at_chip(other):
        return (other * 2 + core, tp)

    def step_to(k):
        return (chip + 11 * k) % CHIPS

    def at_class(other):
        return (chip * 2 + other // 2, other % 2)

    def remote(src, dst, send, recv, device):
        return pltpu.make_async_remote_copy(
            src_ref=src, dst_ref=dst, send_sem=send, recv_sem=recv, device_id=device, device_id_type=MESH
        )

    def wait_for(ref, sem):
        pltpu.make_async_copy(ref, ref, sem).wait()

    peer = (chip * 2 + 1 - core, tp)

    def load_group(g):
        columns = slice(g * D, (g + 1) * D)
        pltpu.make_async_copy(ck.at[:, columns], kcat.at[g, pl.ds(ANCHOR, ROWS)], load_k.at[g]).start()
        pltpu.make_async_copy(
            cv.at[:, columns], vcat.at[g, pl.ds(ANCHOR, ROWS), pl.ds(0, D)], load_v.at[g]
        ).start()

    def load_rows(i):
        pltpu.make_async_copy(cq.at[:, i * HS * D : (i + 1) * HS * D], qv.at[i], load_q.at[i]).start()

    def await_group(g):
        wait_for(kcat.at[g, pl.ds(ANCHOR, ROWS)], load_k.at[g])
        wait_for(vcat.at[g, pl.ds(ANCHOR, ROWS), pl.ds(0, D)], load_v.at[g])

    load_group(0)
    load_rows(0)

    barrier = pltpu.get_barrier_semaphore()

    def greet(k, carry):
        pl.semaphore_signal(barrier, inc=1, device_id=at_chip((chip + k) % CHIPS), device_id_type=MESH)
        return carry

    lax.fori_loop(1, CHIPS, greet, 0)
    for k in range(1, 4):
        pl.semaphore_signal(barrier, inc=1, device_id=at_class((me + k) % 4), device_id_type=MESH)

    small = [
        pltpu.make_async_copy(src, dst, load_s.at[at])
        for at, (src, dst) in enumerate(((sq_in, sq), (sk_in, sk), (sv_in, sv)))
    ]
    for copy in small:
        copy.start()

    for g in range(1, GROUPS):
        load_group(g)
    for i in range(1, FIRST):
        load_rows(i)

    @pl.when(ctx == 0)
    def _():
        for b in range(8):
            source = (ck if b < 4 else cv).at[:ANCHOR, (b % 4) * D : (b % 4 + 1) * D]
            pltpu.make_async_copy(source, anc.at[b * ANCHOR : (b + 1) * ANCHOR], load_a.at[b]).start()

    vcat[:, ANCHOR:, D:] = jnp.ones((GROUPS, ROWS, D), BF)
    await_group(0)

    swaps = []
    for gl in range(2):
        g = (1 - core) * 2 + gl
        swaps.append(
            remote(
                kcat.at[g, pl.ds(ANCHOR, ROWS)], kpeer.at[gl], swap_send.at[gl], swap_recv.at[gl], peer
            )
        )
        swaps.append(
            remote(
                vcat.at[g, pl.ds(ANCHOR, ROWS), pl.ds(0, D)],
                vpeer.at[gl, :, pl.ds(0, D)],
                swap_send.at[2 + gl],
                swap_recv.at[2 + gl],
                peer,
            )
        )

    piece = anc.at[pl.ds(chip * PIECE, PIECE)]

    def scatter(other, carry):
        rows = anc.at[pl.ds(other * PIECE, PIECE)]
        remote(rows, rows, scatter_send, scatter_recv, at_chip(other)).start()
        return carry

    def spread(gl):
        def one(k, carry):
            rows = got.at[gl, chip]
            remote(rows, rows, send1.at[gl], recv1.at[gl], at_chip(step_to(k))).start()
            return carry

        lax.fori_loop(1, CHIPS, one, 0)

    def pass_on(k, carry):
        other = step_to(k)

        @pl.when(other != 0)
        def _():
            remote(piece, piece, anc_send, anc_recv, at_chip(other)).start()

        return carry

    def pass_kv(k, carry):
        rows = gotkv.at[chip]
        remote(rows, rows, send1kv, recv1kv, at_chip(step_to(k))).start()
        return carry

    def give(gl):
        def one(k, carry):
            other = step_to(k)
            at = pl.ds(gl * 4, 4 + gl)
            remote(
                sent.at[other, at], parts.at[chip, at], send2.at[gl], recv2.at[gl], at_chip(other)
            ).start()
            return carry

        lax.fori_loop(1, CHIPS, one, 0)

    def step(s, carry):
        stretch_now = (s == EARLY) | (s == FIRST + 1)

        @pl.when(s == 1)
        def _():
            for copy in small:
                copy.wait()
            held = sq[...].astype(F32)
            for other in range(4):
                for gl in range(2):
                    head = (other % 2) * 32 + (other // 2) * 16 + gl * 8
                    rows = [held[r : r + 1, (head + h) * D : (head + h + 1) * D] for r in range(2) for h in range(8)]
                    cls[other, gl] = jnp.concatenate(rows, 0).astype(BF)
            for b, ref in enumerate((sk, sv)):
                held = ref[...].astype(F32)
                for other in range(2):
                    for gl in range(2):
                        at = (other * 2 + gl) * D
                        kvtiles[other, b * 8 + gl * 4 : b * 8 + gl * 4 + 4, :] = held[:, at : at + D]
            clskv[...] = kvtiles[...].astype(BF)
            for gl in range(2):
                got[gl, chip, me] = cls[me, gl]
            gotkv[chip, core] = clskv[core]

            vcat[:, :ANCHOR, D:] = jnp.ones((GROUPS, ANCHOR, D), BF)
            vpeer[:, :, D:] = jnp.ones((2, ROWS, D), BF)
            pl.semaphore_wait(barrier, CHIPS - 1 + 3)

            for k in range(1, 4):
                other = (me + k) % 4
                remote(cls.at[other], got.at[:, chip, me], send0.at[0], recv0, at_class(other)).start()
            remote(clskv.at[1 - core], gotkv.at[chip, core], send0.at[1], recv0kv, peer).start()

            @pl.when(ctx == 0)
            def _():
                for b in range(8):
                    wait_for(anc.at[b * ANCHOR : (b + 1) * ANCHOR], load_a.at[b])
                lax.fori_loop(1, CHIPS, scatter, 0)

        @pl.when(s == 2)
        def _():
            wait_for(got.at[:, 0, 0:3], recv0)
            spread(0)
            for g in range(1, GROUPS):
                await_group(g)
            for copy in swaps:
                copy.start()

        @pl.when(s == 3)
        def _():
            spread(1)

        @pl.when((s == 4) & (core == 0))
        def _():
            @pl.when(chip != 0)
            def _():
                wait_for(piece, scatter_recv)

            lax.fori_loop(1, CHIPS, pass_on, 0)

        @pl.when(s == FIRST + 1)
        def _():
            wait_for(gotkv.at[0, 0], recv0kv)
            lax.fori_loop(1, CHIPS, pass_kv, 0)

        @pl.when(jnp.logical_not(stretch_now))
        def _():
            i = jnp.where(s > EARLY, s - 1, s)
            wait_for(qv.at[i], load_q.at[i])
            own_step(i, qv, kcat, vcat, part)

        @pl.when(s == EARLY)
        def _():
            for copy in swaps:
                copy.wait_recv()
            wait_for(got.at[0, 0 : CHIPS - 1], recv1.at[0])

        @pl.when(s == FIRST + 1)
        def _():
            wait_for(got.at[1, 0 : CHIPS - 1], recv1.at[1])

            @pl.when(core == 0)
            def _():
                @pl.when(chip != 0)
                def _():
                    wait_for(anc.at[: (CHIPS - 1) * PIECE], anc_recv)

                remote(anc, anc, core_send, core_recv, peer).start()

        @pl.when(stretch_now)
        def _():
            stretch_step((s == FIRST + 1).astype(jnp.int32), core, got, kcat, vcat, kpeer, vpeer, sent, lse)

        return carry

    lax.fori_loop(0, FIRST + 2, step, 0)
    for other in range(CHIPS):
        sent[other, 8] = level_tile(lse[0, other : other + 1, :] + lse[1, other : other + 1, :])
    give(0)
    give(1)

    parts[chip] = sent[chip]

    @pl.when(core == 1)
    def _():
        wait_for(anc, core_recv)

    for g in range(GROUPS):
        kcat[g, :ANCHOR, :] = anc[g * ANCHOR : (g + 1) * ANCHOR, :]
        vcat[g, :ANCHOR, :D] = anc[(GROUPS + g) * ANCHOR : (GROUPS + g + 1) * ANCHOR, :]

    @pl.when(ctx == 0)
    def _():
        for g in range(GROUPS):
            key = kcat[g, ANCHOR : ANCHOR + 16, :].astype(F32)[0:1]
            kcat[g, :ANCHOR, :] = jnp.broadcast_to(key, (ANCHOR, D)).astype(BF)
            vcat[g, :ANCHOR, :] = jnp.zeros((ANCHOR, 2 * D), BF)

    rest = FIRST // 2
    hand = [
        pltpu.make_async_copy(kcat.at[pl.ds(rest, GROUPS - rest)], keys_out, put.at[FIRST]),
        pltpu.make_async_copy(vcat.at[pl.ds(rest, GROUPS - rest)], values_out, put.at[FIRST + 1]),
    ]
    for copy in hand:
        copy.start()

    def anchored(i, carry):
        @pl.when(i == MERGE)
        def _():
            wait_for(gotkv.at[0 : CHIPS - 1], recv1kv)
            self_step(chip, got, gotkv, parts)
            wait_for(parts.at[0 : CHIPS - 1, 0:4], recv2.at[0])
            wait_for(parts.at[0 : CHIPS - 1, 4:9], recv2.at[1])
            merged = merge_step(parts).astype(BF).reshape(2, 4, 16, D)
            for gl in range(2):
                mine[:, gl] = merged[gl]
            for k in range(1, 4):
                other = (me + k) % 4
                remote(mine.at[other], last.at[me], send3, recv3, at_class(other)).start()
            last[me] = mine[me]

        def done(t):
            rows = pl.ds(t * TILE, TILE)
            pltpu.make_async_copy(qv.at[i, rows], out.at[i, rows], put.at[i]).start()

        anchor_step(i, qv, kcat, vcat, part, done)
        return carry

    lax.fori_loop(0, FIRST, anchored, 0)
    wait_for(last.at[0:3], recv3)
    result = pltpu.make_async_copy(last, stretch_out, put.at[FIRST + 2])
    result.start()

    for i in range(FIRST):
        pltpu.make_async_copy(qv.at[i], out.at[i], put.at[i]).wait()
    result.wait()
    for copy in hand:
        copy.wait()
    wait_for(cls.at[0:3], send0.at[0])
    wait_for(clskv.at[0], send0.at[1])
    for copy in swaps:
        copy.wait_send()
    for gl in range(2):
        wait_for(got.at[gl, 0 : CHIPS - 1], send1.at[gl])
    wait_for(gotkv.at[0 : CHIPS - 1], send1kv)
    wait_for(sent.at[0 : CHIPS - 1, 0:4], send2.at[0])
    wait_for(sent.at[0 : CHIPS - 1, 4:9], send2.at[1])
    wait_for(mine.at[0:3], send3)

    @pl.when(ctx == 0)
    def _():
        wait_for(anc.at[: (CHIPS - 1) * PIECE], scatter_send)

    @pl.when(core == 0)
    def _():
        wait_for(anc, core_send)

        @pl.when(chip == 0)
        def _():
            wait_for(anc.at[: (CHIPS - 1) * PIECE], anc_send)

        @pl.when(chip != 0)
        def _():
            wait_for(anc.at[: (CHIPS - 2) * PIECE], anc_send)


def first_call(cq, ck, cv, sq, sk, sv):
    dma = pltpu.SemaphoreType.DMA
    vmem = pltpu.VMEM
    anywhere = pl.BlockSpec(memory_space=pl.ANY)
    rest = GROUPS - FIRST // 2
    return pl.pallas_call(
        first_kernel,
        in_specs=[anywhere] * 6,
        out_specs=[anywhere] * 4,
        out_shape=[
            jax.ShapeDtypeStruct((FIRST, ROWS, HS * D), BF),
            jax.ShapeDtypeStruct((rest, KEYS, D), BF),
            jax.ShapeDtypeStruct((rest, KEYS, 2 * D), BF),
            jax.ShapeDtypeStruct((4, 2, 16, D), BF),
        ],
        scratch_shapes=[
            vmem((2, 64 * D), BF),
            vmem((4, GROUPS * D), BF),
            vmem((4, GROUPS * D), BF),
            vmem((FIRST, ROWS, HS * D), BF),
            vmem((GROUPS, KEYS, D), BF),
            vmem((GROUPS, KEYS, 2 * D), BF),
            vmem((2, ROWS, D), BF),
            vmem((2, ROWS, 2 * D), BF),
            vmem((4, 2, 16, D), BF),
            vmem((2, 16, D), BF),
            vmem((2, CHIPS, 4, 16, D), BF),
            vmem((CHIPS, 2, 16, D), BF),
            vmem((8 * ANCHOR, D), BF),
            vmem((FIRST, TILES, M, 2 * D), F32),
            vmem((CHIPS, 9, 16, D), BF),
            vmem((CHIPS + 1, 9, 16, D), BF),
            vmem((2, CHIPS, D), F32),
            vmem((4, 2, 16, D), BF),
            vmem((4, 2, 16, D), BF),
            vmem((2, 16, D), F32),
            dma((3,)), dma((FIRST,)), dma((GROUPS,)), dma((GROUPS,)), dma((8,)), dma((FIRST + 3,)),
            dma((2,)), dma, dma, dma((4,)), dma((4,)), dma((2,)), dma((2,)), dma, dma,
            dma, dma, dma, dma, dma, dma,
            dma((2,)), dma((2,)), dma, dma,
        ],
        compiler_params=pltpu.CompilerParams(
            collective_id=0, has_side_effects=True, vmem_limit_bytes=58 * 2**20
        ),
        name="gather_stretch_first_heads",
    )(cq, ck, cv, sq, sk, sv)


def second_kernel(q, keys, values, last, before, out, stretch_out, ov, passing, rows_out, put, fetch, carry):
    i = pl.program_id(0)
    fetches = [pltpu.make_async_copy(before.at[j], passing.at[j], fetch.at[j]) for j in range(FIRST)]
    moves = [
        pltpu.make_async_copy(passing.at[j], out.at[:, j * HS * D : (j + 1) * HS * D], carry.at[j])
        for j in range(FIRST)
    ]
    result = pltpu.make_async_copy(rows_out, stretch_out, carry.at[FIRST])

    @pl.when(i == 0)
    def _():
        for copy in fetches:
            copy.start()
        for other in range(4):
            for gl in range(2):
                head = (other % 2) * 32 + (other // 2) * 16 + gl * 8
                held = last[other, gl].astype(F32)
                rows = [
                    jnp.concatenate([held[r * 8 + h : r * 8 + h + 1] for h in range(8)], 1) for r in range(2)
                ]
                rows_out[:, head * D : (head + 8) * D] = jnp.concatenate(rows, 0).astype(BF)
        result.start()

    def columns(step):
        return pl.ds(pl.multiple_of((FIRST + step) * HS * D, HS * D), HS * D)

    def done(t):
        rows = pl.ds(t * TILE, TILE)
        pltpu.make_async_copy(ov.at[i, rows], out.at[rows, columns(i)], put.at[i]).start()

    def between():
        @pl.when(i == 0)
        def _():
            for come, go in zip(fetches, moves):
                come.wait()
                go.start()

    whole_step(q, 0, ov, i, keys, values, 0, done, between)

    @pl.when(i == HALVES - FIRST - 1)
    def _():
        for step in range(HALVES - FIRST):
            pltpu.make_async_copy(ov.at[step], out.at[:, columns(step)], put.at[step]).wait()
        for copy in moves:
            copy.wait()
        result.wait()


def second_call(cq, keys, values, last, before):
    steps = HALVES - FIRST
    base = FIRST // 2

    def group(i):
        return (FIRST + i) // 2

    return pl.pallas_call(
        lambda q, *rest: second_kernel(OneStep(q), *rest),
        grid=(steps,),
        in_specs=[
            pl.BlockSpec((ROWS, HS * D), lambda i: (0, FIRST + i)),
            pl.BlockSpec((1, KEYS, D), lambda i: (group(i) - base, 0, 0)),
            pl.BlockSpec((1, KEYS, 2 * D), lambda i: (group(i) - base, 0, 0)),
            pl.BlockSpec((4, 2, 16, D), lambda i: (0, 0, 0, 0)),
            pl.BlockSpec(memory_space=pl.ANY),
        ],
        out_specs=[pl.BlockSpec(memory_space=pl.ANY), pl.BlockSpec(memory_space=pl.ANY)],
        out_shape=[
            jax.ShapeDtypeStruct((ROWS, 2 * GROUPS * HS * D), BF),
            jax.ShapeDtypeStruct((2, 64 * D), BF),
        ],
        scratch_shapes=[
            pltpu.VMEM((steps, ROWS, HS * D), BF),
            pltpu.VMEM((FIRST, ROWS, HS * D), BF),
            pltpu.VMEM((2, 64 * D), BF),
            pltpu.SemaphoreType.DMA((steps,)),
            pltpu.SemaphoreType.DMA((FIRST,)),
            pltpu.SemaphoreType.DMA((FIRST + 1,)),
        ],
        compiler_params=pltpu.CompilerParams(vmem_limit_bytes=58 * 2**20),
        name="last_heads",
    )(cq, keys, values, last, before)


class OneStep:
    def __init__(self, ref):
        self.ref = ref

    def __getitem__(self, index):
        return self.ref[index[1:]]


def body(cq, ck, cv, sq, sk, sv):
    before, keys, values, last = first_call(cq, ck, cv, sq, sk, sv)
    context_out, stretch_out = second_call(cq, keys, values, last, before)
    return context_out, stretch_out


def solution(mesh):
    in_specs = (
        P("ctx", "tp"),
        P("ctx", "tp"),
        P("ctx", "tp"),
        P(("ctx", "tp"), None),
        P("ctx", "tp"),
        P("ctx", "tp"),
    )
    out_specs = (P("ctx", "tp"), P(("ctx", "tp"), None))
    return jax.shard_map(body, mesh=mesh, in_specs=in_specs, out_specs=out_specs, check_vma=False)
```

```python
import functools

import jax
import jax.numpy as jnp
from jax import lax
from jax.experimental import pallas as pl
from jax.experimental.pallas import tpu as pltpu
from jax.sharding import PartitionSpec as P

MESH = pl.DeviceIdType.MESH
D = 128
ANCHOR = 384
ROWS = 768
KEYS = ANCHOR + ROWS
GROUPS = 4
CHIPS = 32
LOG2E = 1.4426950408889634
C = D**-0.5 * LOG2E
NEG = -1e30
TILE = 128
TILES = ROWS // TILE
DOWN = list(range(TILES))[::-1]
HS = 4
M = HS * TILE
HALVES = 8
FIRST = 7
MERGE = 5
PIECE = 48
PART = CHIPS * PIECE
BF = jnp.bfloat16
F32 = jnp.float32


def scores_of(q, k):
    return lax.dot_general(q, k, (((1,), (1,)), ((), ())), preferred_element_type=F32)


def stacked(ref, i, t):
    rows = slice(t * TILE, (t + 1) * TILE)
    return jnp.concatenate([ref[i, rows, j * D : (j + 1) * D] for j in range(HS)], 0)


def unstack(ref, i, t, value):
    for j in range(HS):
        ref[i, t * TILE : (t + 1) * TILE, j * D : (j + 1) * D] = value[j * TILE : (j + 1) * TILE]


def mask_last(s):
    line = lax.broadcasted_iota(jnp.int32, (TILE, TILE), 0)
    column = lax.broadcasted_iota(jnp.int32, (TILE, TILE), 1)
    seen = column <= line
    n = s.shape[1]
    last = jnp.concatenate(
        [jnp.where(seen, s[j * TILE : (j + 1) * TILE, n - TILE :], NEG) for j in range(HS)], 0
    )
    return last if n == TILE else jnp.concatenate([s[:, : n - TILE], last], 1)


def in_order(items, first, second, between=None):
    s = first(items[0])
    for at, item in enumerate(items):
        if between is not None and at == len(items) // 2:
            between()
        later = first(items[at + 1]) if at + 1 < len(items) else None
        second(item, s)
        s = later


def own_step(i, qv, kcat, vcat, part):
    g = i // 2

    def first(t):
        n = TILE * (t + 1)
        return scores_of(stacked(qv, i, t), kcat[g, ANCHOR : ANCHOR + n, :])

    def second(t, s):
        n = TILE * (t + 1)
        s = mask_last(s)
        m = jnp.max(s, -1, keepdims=True)
        p = jnp.exp2((s - m) * C).astype(BF)
        o = jnp.dot(p, vcat[g, ANCHOR : ANCHOR + n, :], preferred_element_type=F32)
        total = o[:, D:]
        part[i, t, :, :D] = o[:, :D] / total
        part[i, t, :, D:] = m + jnp.log(total) * (LOG2E / C)

    in_order(DOWN, first, second)


def anchor_step(i, qv, kcat, vcat, part, done):
    g = i // 2

    def first(t):
        return scores_of(stacked(qv, i, t), kcat[g, :ANCHOR, :])

    def second(t, s):
        held = part[i, t, :, D:]
        m = jnp.maximum(jnp.max(s, -1, keepdims=True), held)
        p = [jnp.exp2((s[:, j * D : (j + 1) * D] - m) * C).astype(BF) for j in range(ANCHOR // D)]
        o = jnp.dot(jnp.concatenate(p, 1), vcat[g, :ANCHOR, :], preferred_element_type=F32)
        e = jnp.exp2((held - m) * C)
        unstack(qv, i, t, ((o[:, :D] + e * part[i, t, :, :D]) / (o[:, D:] + e)).astype(BF))
        done(t)

    in_order(list(range(TILES)), first, second)


def whole_step(q_ref, i, o_ref, o_at, kcat, vcat, g, done, between):
    def first(t):
        return scores_of(stacked(q_ref, i, t), kcat[g, : ANCHOR + TILE * (t + 1), :])

    def second(t, s):
        s = mask_last(s)
        m = jnp.max(s, -1, keepdims=True)
        p = jnp.exp2((s - m) * C).astype(BF)
        o = jnp.dot(p, vcat[g, : ANCHOR + TILE * (t + 1), :], preferred_element_type=F32)
        unstack(o_ref, o_at, t, (o[:, :D] / o[:, D:]).astype(BF))
        done(t)

    in_order(DOWN, first, second, between)


def stretch_step(gl, chip, core, got, kcat, vcat, kpeer, vpeer, kown, vown, sent, lse):
    g = core * 2 + gl
    near = 8
    size = near * 64
    line = lax.broadcasted_iota(jnp.int32, (64, D), 0)
    column = lax.broadcasted_iota(jnp.int32, (64, D), 1)
    mine = column == line + 64 * gl
    place = lax.broadcasted_iota(jnp.int32, (size, 32), 1)
    row = lax.broadcasted_iota(jnp.int32, (size, 32), 0) // 8
    key = chip * 8 + (place // 16) * 4 + place % 4
    here = (place // 4) % 4 == 2 + gl

    def first(at):
        q = got[gl, at * near : (at + 1) * near].reshape(size, D)
        few = jnp.where(here & (key <= at * 64 + row), scores_of(q, kown[...]), NEG)
        return few, scores_of(q, kcat[g, ANCHOR:, :]), scores_of(q, kpeer[gl])

    def second(at, s):
        m = functools.reduce(jnp.maximum, [jnp.max(part, -1, keepdims=True) for part in s])
        o = jnp.zeros((size, 2 * D), F32)
        for part, value in zip(s, (vown[...], vcat[g, ANCHOR:, :], vpeer[gl])):
            p = jnp.exp2((part - m) * C).astype(BF)
            o = o + jnp.dot(p, value, preferred_element_type=F32)
        total = o[:, D:]
        value = (o[:, :D] / total).astype(BF).reshape(near, 4, 16, D)
        sent[at * near : (at + 1) * near, pl.ds(gl * 4, 4)] = value
        level = m * C + jnp.log(total) * LOG2E
        level = jnp.where(mine[None], level.reshape(near, 64, D), 0.0)
        lse[gl, at * near : (at + 1) * near, :] = jnp.sum(level, axis=1)

    in_order(list(range(CHIPS // near)), first, second)


def level_tile(level):
    high = level.astype(BF).astype(F32)
    middle = (level - high).astype(BF).astype(F32)
    low = level - high - middle
    row = lax.broadcasted_iota(jnp.int32, (16, D), 0)
    tile = jnp.where(row == 0, high, jnp.where(row == 1, middle, jnp.where(row == 2, low, 0.0)))
    return tile.astype(BF)


def merge_step(parts):
    def level_of(s):
        tile = parts[s, 8].astype(F32)
        return tile[0:1] + tile[1:2] + tile[2:3]

    levels = [level_of(s) for s in range(CHIPS)]
    top = functools.reduce(jnp.maximum, levels)
    weights = [jnp.exp2(level - top) for level in levels]
    total = functools.reduce(jnp.add, weights)
    line = lax.broadcasted_iota(jnp.int32, (D, D), 0)
    column = lax.broadcasted_iota(jnp.int32, (D, D), 1)
    same = line == column
    result = jnp.zeros((D, D), F32)
    for s in range(CHIPS):
        factor = jnp.sum(jnp.where(same, weights[s] / total, 0.0), -1, keepdims=True)
        result = result + factor * parts[s, 0:8].astype(F32).reshape(D, D)
    return result


def first_kernel(
    cq, ck, cv, sq_in, sk_in, sv_in,
    out, keys_out, values_out, stretch_out,
    sq, sk, sv, qv, kcat, vcat, kpeer, vpeer, cls, clskv, got, gotkv, kown, vown, anc, part, sent, parts, lse, mine, last, kvtiles,
    load_s, load_q, load_k, load_v, load_a, put,
    send0, recv0, recv0kv, swap_send, swap_recv, send1, recv1,
    scatter_send, scatter_recv, anc_send, anc_recv, core_send, core_recv,
    send2, recv2, send3, recv3,
):
    ctx, tp = lax.axis_index("ctx"), lax.axis_index("tp")
    chip, core = ctx // 2, ctx % 2
    me = core * 2 + tp

    def at_chip(other):
        return (other * 2 + core, tp)

    def step_to(k):
        return (chip + 11 * k) % CHIPS

    def at_class(other):
        return (chip * 2 + other // 2, other % 2)

    def remote(src, dst, send, recv, device):
        return pltpu.make_async_remote_copy(
            src_ref=src, dst_ref=dst, send_sem=send, recv_sem=recv, device_id=device, device_id_type=MESH
        )

    def wait_for(ref, sem):
        pltpu.make_async_copy(ref, ref, sem).wait()

    peer = (chip * 2 + 1 - core, tp)

    def load_group(g):
        columns = slice(g * D, (g + 1) * D)
        pltpu.make_async_copy(ck.at[:, columns], kcat.at[g, pl.ds(ANCHOR, ROWS)], load_k.at[g]).start()
        pltpu.make_async_copy(
            cv.at[:, columns], vcat.at[g, pl.ds(ANCHOR, ROWS), pl.ds(0, D)], load_v.at[g]
        ).start()

    def load_rows(i):
        pltpu.make_async_copy(cq.at[:, i * HS * D : (i + 1) * HS * D], qv.at[i], load_q.at[i]).start()

    def await_group(g):
        wait_for(kcat.at[g, pl.ds(ANCHOR, ROWS)], load_k.at[g])
        wait_for(vcat.at[g, pl.ds(ANCHOR, ROWS), pl.ds(0, D)], load_v.at[g])

    load_group(0)
    load_rows(0)

    barrier = pltpu.get_barrier_semaphore()

    def greet(k, carry):
        pl.semaphore_signal(barrier, inc=1, device_id=at_chip((chip + k) % CHIPS), device_id_type=MESH)
        return carry

    lax.fori_loop(1, CHIPS, greet, 0)

    @pl.when((core == 1) & (chip != 0))
    def _():
        pl.semaphore_signal(barrier, inc=1, device_id=(0, tp), device_id_type=MESH)

    for k in range(1, 4):
        pl.semaphore_signal(barrier, inc=1, device_id=at_class((me + k) % 4), device_id_type=MESH)

    small = [
        pltpu.make_async_copy(src, dst, load_s.at[at])
        for at, (src, dst) in enumerate(((sq_in, sq), (sk_in, sk), (sv_in, sv)))
    ]
    for copy in small:
        copy.start()

    for g in range(1, GROUPS):
        load_group(g)
    for i in range(1, FIRST):
        load_rows(i)

    @pl.when(ctx == 0)
    def _():
        for b in range(8):
            source = (ck if b < 4 else cv).at[:ANCHOR, (b % 4) * D : (b % 4 + 1) * D]
            pltpu.make_async_copy(source, anc.at[b * ANCHOR : (b + 1) * ANCHOR], load_a.at[b]).start()

    vcat[:, ANCHOR:, D:] = jnp.ones((GROUPS, ROWS, D), BF)
    await_group(0)

    swaps = []
    for gl in range(2):
        g = (1 - core) * 2 + gl
        swaps.append(
            remote(
                kcat.at[g, pl.ds(ANCHOR, ROWS)], kpeer.at[gl], swap_send.at[gl], swap_recv.at[gl], peer
            )
        )
        swaps.append(
            remote(
                vcat.at[g, pl.ds(ANCHOR, ROWS), pl.ds(0, D)],
                vpeer.at[gl, :, pl.ds(0, D)],
                swap_send.at[2 + gl],
                swap_recv.at[2 + gl],
                peer,
            )
        )

    piece = anc.at[pl.ds(core * PART + chip * PIECE, PIECE)]
    half = anc.at[pl.ds(core * PART, PART)]

    def scatter(other, carry):
        rows = anc.at[pl.ds((other % 2) * PART + (other // 2) * PIECE, PIECE)]
        remote(rows, rows, scatter_send, scatter_recv, (other, tp)).start()
        return carry

    def spread(gl):
        def one(k, carry):
            rows = got.at[gl, chip]
            remote(rows, rows, send1.at[gl], recv1.at[gl], at_chip(step_to(k))).start()
            return carry

        lax.fori_loop(1, CHIPS, one, 0)

    def pass_on(k, carry):
        other = step_to(k)

        @pl.when((other != 0) | (core != 0))
        def _():
            remote(piece, piece, anc_send, anc_recv, at_chip(other)).start()

        return carry

    def give(gl):
        def one(k, carry):
            other = step_to(k)
            at = pl.ds(gl * 4, 4 + gl)
            remote(
                sent.at[other, at], parts.at[chip, at], send2.at[gl], recv2.at[gl], at_chip(other)
            ).start()
            return carry

        lax.fori_loop(1, CHIPS, one, 0)

    def step(s, carry):
        stretch_now = s >= FIRST

        @pl.when(s == 1)
        def _():
            for copy in small:
                copy.wait()
            held = sq[...].astype(F32)
            for other in range(4):
                for gl in range(2):
                    head = (other % 2) * 32 + (other // 2) * 16 + gl * 8
                    rows = [held[r : r + 1, (head + h) * D : (head + h + 1) * D] for r in range(2) for h in range(8)]
                    cls[other, gl] = jnp.concatenate(rows, 0).astype(BF)
            for b, ref in enumerate((sk, sv)):
                held = ref[...].astype(F32)
                for other in range(2):
                    for gl in range(2):
                        at = (other * 2 + gl) * D
                        kvtiles[other, b * 8 + gl * 4 : b * 8 + gl * 4 + 4, :] = held[:, at : at + D]
            clskv[...] = kvtiles[...].astype(BF)
            for gl in range(2):
                got[gl, chip, me] = cls[me, gl]
            gotkv[core] = clskv[core]

            vcat[:, :ANCHOR, D:] = jnp.ones((GROUPS, ANCHOR, D), BF)
            vpeer[:, :, D:] = jnp.ones((2, ROWS, D), BF)
            pl.semaphore_wait(barrier, CHIPS - 1 + 3 + jnp.where(ctx == 0, CHIPS - 1, 0))


            for k in range(1, 4):
                other = (me + k) % 4
                remote(cls.at[other], got.at[:, chip, me], send0.at[0], recv0, at_class(other)).start()
            remote(clskv.at[1 - core], gotkv.at[core], send0.at[1], recv0kv, peer).start()

            @pl.when(ctx == 0)
            def _():
                for b in range(8):
                    wait_for(anc.at[b * ANCHOR : (b + 1) * ANCHOR], load_a.at[b])
                lax.fori_loop(1, 2 * CHIPS, scatter, 0)

        @pl.when(s == 2)
        def _():
            wait_for(got.at[:, 0, 0:3], recv0)
            spread(0)
            spread(1)
            for g in range(1, GROUPS):
                await_group(g)
            for copy in swaps:
                copy.start()

        @pl.when(s == 4)
        def _():
            @pl.when(ctx != 0)
            def _():
                wait_for(piece, scatter_recv)

            lax.fori_loop(1, CHIPS, pass_on, 0)

        @pl.when(s < FIRST)
        def _():
            wait_for(qv.at[s], load_q.at[s])
            own_step(s, qv, kcat, vcat, part)

        @pl.when(s == FIRST)
        def _():
            wait_for(gotkv.at[0], recv0kv)
            held = gotkv[...].astype(F32)
            kown[...] = jnp.concatenate([held[:, 8:], held[:, :8]], 1).astype(BF).reshape(32, D)
            vown[:, :D] = gotkv[...].reshape(32, D)
            vown[:, D:] = jnp.ones((32, D), BF)
            for copy in swaps:
                copy.wait_recv()
            wait_for(got.at[0, 0 : CHIPS - 1], recv1.at[0])

        @pl.when(s == FIRST + 1)
        def _():
            wait_for(got.at[1, 0 : CHIPS - 1], recv1.at[1])

            give(0)

        @pl.when(stretch_now)
        def _():
            stretch_step(s - FIRST, chip, core, got, kcat, vcat, kpeer, vpeer, kown, vown, sent, lse)

        return carry

    lax.fori_loop(0, FIRST + 2, step, 0)
    for other in range(CHIPS):
        sent[other, 8] = level_tile(lse[0, other : other + 1, :] + lse[1, other : other + 1, :])

    @pl.when(ctx != 0)
    def _():
        wait_for(anc.at[0 : (CHIPS - 1) * PIECE], anc_recv)

    @pl.when(ctx != 1)
    def _():
        remote(half, half, core_send, core_recv, peer).start()

    give(1)

    parts[chip] = sent[chip]

    @pl.when(ctx != 0)
    def _():
        wait_for(half, core_recv)

    for g in range(GROUPS):
        kcat[g, :ANCHOR, :] = anc[g * ANCHOR : (g + 1) * ANCHOR, :]
        vcat[g, :ANCHOR, :D] = anc[(GROUPS + g) * ANCHOR : (GROUPS + g + 1) * ANCHOR, :]

    @pl.when(ctx == 0)
    def _():
        for g in range(GROUPS):
            key = kcat[g, ANCHOR : ANCHOR + 16, :].astype(F32)[0:1]
            kcat[g, :ANCHOR, :] = jnp.broadcast_to(key, (ANCHOR, D)).astype(BF)
            vcat[g, :ANCHOR, :] = jnp.zeros((ANCHOR, 2 * D), BF)

    rest = FIRST // 2
    hand = [
        pltpu.make_async_copy(kcat.at[pl.ds(rest, GROUPS - rest)], keys_out, put.at[FIRST]),
        pltpu.make_async_copy(vcat.at[pl.ds(rest, GROUPS - rest)], values_out, put.at[FIRST + 1]),
    ]
    for copy in hand:
        copy.start()

    def anchored(i, carry):
        @pl.when(i == MERGE)
        def _():
            wait_for(parts.at[0 : CHIPS - 1, 0:4], recv2.at[0])
            wait_for(parts.at[0 : CHIPS - 1, 4:9], recv2.at[1])
            merged = merge_step(parts).astype(BF).reshape(2, 4, 16, D)
            for gl in range(2):
                mine[:, gl] = merged[gl]
            for k in range(1, 4):
                other = (me + k) % 4
                remote(mine.at[other], last.at[me], send3, recv3, at_class(other)).start()
            last[me] = mine[me]

        def done(t):
            rows = pl.ds(t * TILE, TILE)
            pltpu.make_async_copy(qv.at[i, rows], out.at[i, rows], put.at[i]).start()

        anchor_step(i, qv, kcat, vcat, part, done)
        return carry

    lax.fori_loop(0, FIRST, anchored, 0)
    wait_for(last.at[0:3], recv3)
    result = pltpu.make_async_copy(last, stretch_out, put.at[FIRST + 2])
    result.start()

    for i in range(FIRST):
        pltpu.make_async_copy(qv.at[i], out.at[i], put.at[i]).wait()
    result.wait()
    for copy in hand:
        copy.wait()
    wait_for(cls.at[0:3], send0.at[0])
    wait_for(clskv.at[0], send0.at[1])
    for copy in swaps:
        copy.wait_send()
    for gl in range(2):
        wait_for(got.at[gl, 0 : CHIPS - 1], send1.at[gl])
    wait_for(sent.at[0 : CHIPS - 1, 0:4], send2.at[0])
    wait_for(sent.at[0 : CHIPS - 1, 4:9], send2.at[1])
    wait_for(mine.at[0:3], send3)

    @pl.when(ctx == 0)
    def _():
        wait_for(anc.at[0 : (2 * CHIPS - 1) * PIECE], scatter_send)

    @pl.when(ctx != 1)
    def _():
        wait_for(half, core_send)

    @pl.when((chip == 0) | (core == 1))
    def _():
        wait_for(anc.at[0 : (CHIPS - 1) * PIECE], anc_send)

    @pl.when((chip != 0) & (core == 0))
    def _():
        wait_for(anc.at[0 : (CHIPS - 2) * PIECE], anc_send)


def first_call(cq, ck, cv, sq, sk, sv):
    dma = pltpu.SemaphoreType.DMA
    vmem = pltpu.VMEM
    anywhere = pl.BlockSpec(memory_space=pl.ANY)
    rest = GROUPS - FIRST // 2
    return pl.pallas_call(
        first_kernel,
        in_specs=[anywhere] * 6,
        out_specs=[anywhere] * 4,
        out_shape=[
            jax.ShapeDtypeStruct((FIRST, ROWS, HS * D), BF),
            jax.ShapeDtypeStruct((rest, KEYS, D), BF),
            jax.ShapeDtypeStruct((rest, KEYS, 2 * D), BF),
            jax.ShapeDtypeStruct((4, 2, 16, D), BF),
        ],
        scratch_shapes=[
            vmem((2, 64 * D), BF),
            vmem((4, GROUPS * D), BF),
            vmem((4, GROUPS * D), BF),
            vmem((FIRST, ROWS, HS * D), BF),
            vmem((GROUPS, KEYS, D), BF),
            vmem((GROUPS, KEYS, 2 * D), BF),
            vmem((2, ROWS, D), BF),
            vmem((2, ROWS, 2 * D), BF),
            vmem((4, 2, 16, D), BF),
            vmem((2, 16, D), BF),
            vmem((2, CHIPS, 4, 16, D), BF),
            vmem((2, 16, D), BF),
            vmem((32, D), BF),
            vmem((32, 2 * D), BF),
            vmem((8 * ANCHOR, D), BF),
            vmem((FIRST, TILES, M, 2 * D), F32),
            vmem((CHIPS, 9, 16, D), BF),
            vmem((CHIPS, 9, 16, D), BF),
            vmem((2, CHIPS, D), F32),
            vmem((4, 2, 16, D), BF),
            vmem((4, 2, 16, D), BF),
            vmem((2, 16, D), F32),
            dma((3,)), dma((FIRST,)), dma((GROUPS,)), dma((GROUPS,)), dma((8,)), dma((FIRST + 3,)),
            dma((2,)), dma, dma, dma((4,)), dma((4,)), dma((2,)), dma((2,)),
            dma, dma, dma, dma, dma, dma,
            dma((2,)), dma((2,)), dma, dma,
        ],
        compiler_params=pltpu.CompilerParams(
            collective_id=0, has_side_effects=True, vmem_limit_bytes=58 * 2**20
        ),
        name="gather_stretch_first_heads",
    )(cq, ck, cv, sq, sk, sv)


def second_kernel(q, keys, values, last, before, out, stretch_out, ov, passing, rows_out, put, fetch, carry):
    i = pl.program_id(0)
    fetches = [pltpu.make_async_copy(before.at[j], passing.at[j], fetch.at[j]) for j in range(FIRST)]
    moves = [
        pltpu.make_async_copy(passing.at[j], out.at[:, j * HS * D : (j + 1) * HS * D], carry.at[j])
        for j in range(FIRST)
    ]
    result = pltpu.make_async_copy(rows_out, stretch_out, carry.at[FIRST])

    @pl.when(i == 0)
    def _():
        for copy in fetches:
            copy.start()
        for other in range(4):
            for gl in range(2):
                head = (other % 2) * 32 + (other // 2) * 16 + gl * 8
                held = last[other, gl].astype(F32)
                rows = [
                    jnp.concatenate([held[r * 8 + h : r * 8 + h + 1] for h in range(8)], 1) for r in range(2)
                ]
                rows_out[:, head * D : (head + 8) * D] = jnp.concatenate(rows, 0).astype(BF)
        result.start()

    def columns(step):
        return pl.ds(pl.multiple_of((FIRST + step) * HS * D, HS * D), HS * D)

    def done(t):
        rows = pl.ds(t * TILE, TILE)
        pltpu.make_async_copy(ov.at[i, rows], out.at[rows, columns(i)], put.at[i]).start()

    def between():
        @pl.when(i == 0)
        def _():
            for come, go in zip(fetches, moves):
                come.wait()
                go.start()

    @pl.when(lax.axis_index("ctx") >= 0)
    def _():
        whole_step(q, 0, ov, i, keys, values, 0, done, between)

    @pl.when(i == HALVES - FIRST - 1)
    def _():
        for step in range(HALVES - FIRST):
            pltpu.make_async_copy(ov.at[step], out.at[:, columns(step)], put.at[step]).wait()
        for copy in moves:
            copy.wait()
        result.wait()


def second_call(cq, keys, values, last, before):
    steps = HALVES - FIRST
    base = FIRST // 2

    def group(i):
        return (FIRST + i) // 2

    return pl.pallas_call(
        lambda q, *rest: second_kernel(OneStep(q), *rest),
        grid=(steps,),
        in_specs=[
            pl.BlockSpec((ROWS, HS * D), lambda i: (0, FIRST + i)),
            pl.BlockSpec((1, KEYS, D), lambda i: (group(i) - base, 0, 0)),
            pl.BlockSpec((1, KEYS, 2 * D), lambda i: (group(i) - base, 0, 0)),
            pl.BlockSpec((4, 2, 16, D), lambda i: (0, 0, 0, 0)),
            pl.BlockSpec(memory_space=pl.ANY),
        ],
        out_specs=[pl.BlockSpec(memory_space=pl.ANY), pl.BlockSpec(memory_space=pl.ANY)],
        out_shape=[
            jax.ShapeDtypeStruct((ROWS, 2 * GROUPS * HS * D), BF),
            jax.ShapeDtypeStruct((2, 64 * D), BF),
        ],
        scratch_shapes=[
            pltpu.VMEM((steps, ROWS, HS * D), BF),
            pltpu.VMEM((FIRST, ROWS, HS * D), BF),
            pltpu.VMEM((2, 64 * D), BF),
            pltpu.SemaphoreType.DMA((steps,)),
            pltpu.SemaphoreType.DMA((FIRST,)),
            pltpu.SemaphoreType.DMA((FIRST + 1,)),
        ],
        compiler_params=pltpu.CompilerParams(vmem_limit_bytes=58 * 2**20),
        name="last_heads",
    )(cq, keys, values, last, before)


class OneStep:
    def __init__(self, ref):
        self.ref = ref

    def __getitem__(self, index):
        return self.ref[index[1:]]


def body(cq, ck, cv, sq, sk, sv):
    before, keys, values, last = first_call(cq, ck, cv, sq, sk, sv)
    context_out, stretch_out = second_call(cq, keys, values, last, before)
    return context_out, stretch_out


def solution(mesh):
    in_specs = (
        P("ctx", "tp"),
        P("ctx", "tp"),
        P("ctx", "tp"),
        P(("ctx", "tp"), None),
        P("ctx", "tp"),
        P("ctx", "tp"),
    )
    out_specs = (P("ctx", "tp"), P(("ctx", "tp"), None))
    return jax.shard_map(body, mesh=mesh, in_specs=in_specs, out_specs=out_specs, check_vma=False)
```

```python
import functools

import jax
import jax.numpy as jnp
from jax import lax
from jax.experimental import pallas as pl
from jax.experimental.pallas import tpu as pltpu
from jax.sharding import PartitionSpec as P

MESH = pl.DeviceIdType.MESH
D = 128
ANCHOR = 384
ROWS = 768
KEYS = ANCHOR + ROWS
GROUPS = 4
CHIPS = 32
LOG2E = 1.4426950408889634
C = D**-0.5 * LOG2E
NEG = -1e30
TILE = 128
TILES = ROWS // TILE
DOWN = list(range(TILES))[::-1]
HS = 4
M = HS * TILE
HALVES = 8
FIRST = 7
SINGLE = 3
PASS = 1
MERGE = 2
PIECE = 48
PART = CHIPS * PIECE
BF = jnp.bfloat16
F32 = jnp.float32


def scores_of(q, k):
    return lax.dot_general(q, k, (((1,), (1,)), ((), ())), preferred_element_type=F32)


def stacked(ref, i, t):
    rows = slice(t * TILE, (t + 1) * TILE)
    return jnp.concatenate([ref[i, rows, j * D : (j + 1) * D] for j in range(HS)], 0)


def unstack(ref, i, t, value):
    for j in range(HS):
        ref[i, t * TILE : (t + 1) * TILE, j * D : (j + 1) * D] = value[j * TILE : (j + 1) * TILE]


def mask_last(s):
    line = lax.broadcasted_iota(jnp.int32, (TILE, TILE), 0)
    column = lax.broadcasted_iota(jnp.int32, (TILE, TILE), 1)
    seen = column <= line
    n = s.shape[1]
    last = jnp.concatenate(
        [jnp.where(seen, s[j * TILE : (j + 1) * TILE, n - TILE :], NEG) for j in range(HS)], 0
    )
    return last if n == TILE else jnp.concatenate([s[:, : n - TILE], last], 1)


def in_order(items, first, second, between=None):
    s = first(items[0])
    for at, item in enumerate(items):
        if between is not None and at == len(items) // 2:
            between()
        later = first(items[at + 1]) if at + 1 < len(items) else None
        second(item, s)
        s = later


def own_step(steps, qv, kcat, vcat, part):
    def first(item):
        i, t = item
        return scores_of(stacked(qv, i, t), kcat[i // 2, ANCHOR : ANCHOR + TILE * (t + 1), :])

    def second(item, s):
        i, t = item
        s = mask_last(s)
        m = jnp.max(s, -1, keepdims=True)
        p = jnp.exp2((s - m) * C).astype(BF)
        o = jnp.dot(p, vcat[i // 2, ANCHOR : ANCHOR + TILE * (t + 1), :], preferred_element_type=F32)
        total = o[:, D:]
        part[i, t, :, :D] = o[:, :D] / total
        part[i, t, :, D:] = m + jnp.log(total) * (LOG2E / C)

    in_order([(i, t) for i in steps for t in DOWN], first, second)


def anchor_step(steps, qv, kcat, vcat, part, done):
    def first(item):
        i, t = item
        return scores_of(stacked(qv, i, t), kcat[i // 2, :ANCHOR, :])

    def second(item, s):
        i, t = item
        held = part[i, t, :, D:]
        m = jnp.maximum(jnp.max(s, -1, keepdims=True), held)
        p = [jnp.exp2((s[:, j * D : (j + 1) * D] - m) * C).astype(BF) for j in range(ANCHOR // D)]
        o = jnp.dot(jnp.concatenate(p, 1), vcat[i // 2, :ANCHOR, :], preferred_element_type=F32)
        e = jnp.exp2((held - m) * C)
        unstack(qv, i, t, ((o[:, :D] + e * part[i, t, :, :D]) / (o[:, D:] + e)).astype(BF))
        done(i, t)

    in_order([(i, t) for i in steps for t in DOWN], first, second)


def whole_step(q_ref, i, o_ref, o_at, kcat, vcat, g, done, between):
    def first(t):
        return scores_of(stacked(q_ref, i, t), kcat[g, : ANCHOR + TILE * (t + 1), :])

    def second(t, s):
        s = mask_last(s)
        m = jnp.max(s, -1, keepdims=True)
        p = jnp.exp2((s - m) * C).astype(BF)
        o = jnp.dot(p, vcat[g, : ANCHOR + TILE * (t + 1), :], preferred_element_type=F32)
        unstack(o_ref, o_at, t, (o[:, :D] / o[:, D:]).astype(BF))
        done(t)

    in_order(DOWN, first, second, between)


def stretch_step(gl, chip, core, got, kcat, vcat, kpeer, vpeer, kown, vown, sent, lse):
    g = core * 2 + gl
    near = 8
    size = near * 64
    line = lax.broadcasted_iota(jnp.int32, (64, D), 0)
    column = lax.broadcasted_iota(jnp.int32, (64, D), 1)
    mine = column == line + 64 * gl
    place = lax.broadcasted_iota(jnp.int32, (size, 32), 1)
    row = lax.broadcasted_iota(jnp.int32, (size, 32), 0) // 8
    key = chip * 8 + (place // 16) * 4 + place % 4
    here = (place // 4) % 4 == 2 + gl

    def first(at):
        q = got[gl, at * near : (at + 1) * near].reshape(size, D)
        few = jnp.where(here & (key <= at * 64 + row), scores_of(q, kown[...]), NEG)
        return few, scores_of(q, kcat[g, ANCHOR:, :]), scores_of(q, kpeer[gl])

    def second(at, s):
        m = functools.reduce(jnp.maximum, [jnp.max(part, -1, keepdims=True) for part in s])
        o = jnp.zeros((size, 2 * D), F32)
        for part, value in zip(s, (vown[...], vcat[g, ANCHOR:, :], vpeer[gl])):
            p = jnp.exp2((part - m) * C).astype(BF)
            o = o + jnp.dot(p, value, preferred_element_type=F32)
        total = o[:, D:]
        value = (o[:, :D] / total).astype(BF).reshape(near, 4, 16, D)
        sent[at * near : (at + 1) * near, pl.ds(gl * 4, 4)] = value
        level = m * C + jnp.log(total) * LOG2E
        level = jnp.where(mine[None], level.reshape(near, 64, D), 0.0)
        lse[gl, at * near : (at + 1) * near, :] = jnp.sum(level, axis=1)

    in_order(list(range(CHIPS // near)), first, second)


def level_tile(level):
    high = level.astype(BF).astype(F32)
    middle = (level - high).astype(BF).astype(F32)
    low = level - high - middle
    row = lax.broadcasted_iota(jnp.int32, (16, D), 0)
    tile = jnp.where(row == 0, high, jnp.where(row == 1, middle, jnp.where(row == 2, low, 0.0)))
    return tile.astype(BF)


def merge_step(parts):
    def level_of(s):
        tile = parts[s, 8].astype(F32)
        return tile[0:1] + tile[1:2] + tile[2:3]

    levels = [level_of(s) for s in range(CHIPS)]
    top = functools.reduce(jnp.maximum, levels)
    weights = [jnp.exp2(level - top) for level in levels]
    total = functools.reduce(jnp.add, weights)
    line = lax.broadcasted_iota(jnp.int32, (D, D), 0)
    column = lax.broadcasted_iota(jnp.int32, (D, D), 1)
    same = line == column
    result = jnp.zeros((D, D), F32)
    for s in range(CHIPS):
        factor = jnp.sum(jnp.where(same, weights[s] / total, 0.0), -1, keepdims=True)
        result = result + factor * parts[s, 0:8].astype(F32).reshape(D, D)
    return result


def first_kernel(
    cq, ck, cv, sq_in, sk_in, sv_in,
    out, keys_out, values_out, stretch_out,
    sq, sk, sv, qv, kcat, vcat, kpeer, vpeer, cls, clskv, got, gotkv, kown, vown, anc, part, sent, parts, lse, mine, last, kvtiles,
    load_s, load_q, load_k, load_v, load_a, put,
    send0, recv0, recv0kv, swap_send, swap_recv, send1, recv1,
    scatter_send, scatter_recv, anc_send, anc_recv, core_send, core_recv,
    send2, recv2, send3, recv3,
):
    ctx, tp = lax.axis_index("ctx"), lax.axis_index("tp")
    chip, core = ctx // 2, ctx % 2
    me = core * 2 + tp

    def at_chip(other):
        return (other * 2 + core, tp)

    def step_to(k):
        return (chip + 11 * k) % CHIPS

    def at_class(other):
        return (chip * 2 + other // 2, other % 2)

    def remote(src, dst, send, recv, device):
        return pltpu.make_async_remote_copy(
            src_ref=src, dst_ref=dst, send_sem=send, recv_sem=recv, device_id=device, device_id_type=MESH
        )

    def wait_for(ref, sem):
        pltpu.make_async_copy(ref, ref, sem).wait()

    peer = (chip * 2 + 1 - core, tp)

    def load_group(g):
        columns = slice(g * D, (g + 1) * D)
        pltpu.make_async_copy(ck.at[:, columns], kcat.at[g, pl.ds(ANCHOR, ROWS)], load_k.at[g]).start()
        pltpu.make_async_copy(
            cv.at[:, columns], vcat.at[g, pl.ds(ANCHOR, ROWS), pl.ds(0, D)], load_v.at[g]
        ).start()

    def load_rows(i):
        pltpu.make_async_copy(cq.at[:, i * HS * D : (i + 1) * HS * D], qv.at[i], load_q.at[i]).start()

    def await_group(g):
        wait_for(kcat.at[g, pl.ds(ANCHOR, ROWS)], load_k.at[g])
        wait_for(vcat.at[g, pl.ds(ANCHOR, ROWS), pl.ds(0, D)], load_v.at[g])

    load_group(0)
    load_rows(0)

    barrier = pltpu.get_barrier_semaphore()

    def greet(k, carry):
        pl.semaphore_signal(barrier, inc=1, device_id=at_chip((chip + k) % CHIPS), device_id_type=MESH)
        return carry

    lax.fori_loop(1, CHIPS, greet, 0)

    @pl.when((core == 1) & (chip != 0))
    def _():
        pl.semaphore_signal(barrier, inc=1, device_id=(0, tp), device_id_type=MESH)

    for k in range(1, 4):
        pl.semaphore_signal(barrier, inc=1, device_id=at_class((me + k) % 4), device_id_type=MESH)

    small = [
        pltpu.make_async_copy(src, dst, load_s.at[at])
        for at, (src, dst) in enumerate(((sq_in, sq), (sk_in, sk), (sv_in, sv)))
    ]
    for copy in small:
        copy.start()

    for g in range(1, GROUPS):
        load_group(g)
    for i in range(1, FIRST):
        load_rows(i)

    @pl.when(ctx == 0)
    def _():
        for b in range(8):
            source = (ck if b < 4 else cv).at[:ANCHOR, (b % 4) * D : (b % 4 + 1) * D]
            pltpu.make_async_copy(source, anc.at[b * ANCHOR : (b + 1) * ANCHOR], load_a.at[b]).start()

    vcat[:, ANCHOR:, D:] = jnp.ones((GROUPS, ROWS, D), BF)
    await_group(0)

    swaps = []
    for gl in range(2):
        g = (1 - core) * 2 + gl
        swaps.append(
            remote(
                kcat.at[g, pl.ds(ANCHOR, ROWS)], kpeer.at[gl], swap_send.at[gl], swap_recv.at[gl], peer
            )
        )
        swaps.append(
            remote(
                vcat.at[g, pl.ds(ANCHOR, ROWS), pl.ds(0, D)],
                vpeer.at[gl, :, pl.ds(0, D)],
                swap_send.at[2 + gl],
                swap_recv.at[2 + gl],
                peer,
            )
        )

    piece = anc.at[pl.ds(core * PART + chip * PIECE, PIECE)]
    half = anc.at[pl.ds(core * PART, PART)]

    def scatter(other, carry):
        rows = anc.at[pl.ds((other % 2) * PART + (other // 2) * PIECE, PIECE)]
        remote(rows, rows, scatter_send, scatter_recv, (other, tp)).start()
        return carry

    def spread(gl):
        def one(k, carry):
            rows = got.at[gl, chip]
            remote(rows, rows, send1.at[gl], recv1.at[gl], at_chip(step_to(k))).start()
            return carry

        lax.fori_loop(1, CHIPS, one, 0)

    def pass_on(k, carry):
        other = step_to(k)

        @pl.when((other != 0) | (core != 0))
        def _():
            remote(piece, piece, anc_send, anc_recv, at_chip(other)).start()

        return carry

    def give(gl):
        def one(k, carry):
            other = step_to(k)
            at = pl.ds(gl * 4, 4 + gl)
            remote(
                sent.at[other, at], parts.at[chip, at], send2.at[gl], recv2.at[gl], at_chip(other)
            ).start()
            return carry

        lax.fori_loop(1, CHIPS, one, 0)

    def step(s, carry):
        @pl.when(s == 1)
        def _():
            for copy in small:
                copy.wait()
            held = sq[...].astype(F32)
            for other in range(4):
                for gl in range(2):
                    head = (other % 2) * 32 + (other // 2) * 16 + gl * 8
                    rows = [held[r : r + 1, (head + h) * D : (head + h + 1) * D] for r in range(2) for h in range(8)]
                    cls[other, gl] = jnp.concatenate(rows, 0).astype(BF)
            for b, ref in enumerate((sk, sv)):
                held = ref[...].astype(F32)
                for other in range(2):
                    for gl in range(2):
                        at = (other * 2 + gl) * D
                        kvtiles[other, b * 8 + gl * 4 : b * 8 + gl * 4 + 4, :] = held[:, at : at + D]
            clskv[...] = kvtiles[...].astype(BF)
            for gl in range(2):
                got[gl, chip, me] = cls[me, gl]
            gotkv[core] = clskv[core]

            vcat[:, :ANCHOR, D:] = jnp.ones((GROUPS, ANCHOR, D), BF)
            vpeer[:, :, D:] = jnp.ones((2, ROWS, D), BF)
            pl.semaphore_wait(barrier, CHIPS - 1 + 3 + jnp.where(ctx == 0, CHIPS - 1, 0))


            for k in range(1, 4):
                other = (me + k) % 4
                remote(cls.at[other], got.at[:, chip, me], send0.at[0], recv0, at_class(other)).start()
            remote(clskv.at[1 - core], gotkv.at[core], send0.at[1], recv0kv, peer).start()

            @pl.when(ctx == 0)
            def _():
                for b in range(8):
                    wait_for(anc.at[b * ANCHOR : (b + 1) * ANCHOR], load_a.at[b])
                lax.fori_loop(1, 2 * CHIPS, scatter, 0)

        @pl.when(s == 2)
        def _():
            wait_for(got.at[:, 0, 0:3], recv0)
            spread(0)
            spread(1)
            for g in range(1, GROUPS):
                await_group(g)
            for copy in swaps:
                copy.start()

        wait_for(qv.at[s], load_q.at[s])
        own_step([s], qv, kcat, vcat, part)
        return carry

    lax.fori_loop(0, SINGLE, step, 0)

    def pair(j, carry):
        @pl.when(j == PASS)
        def _():
            @pl.when(ctx != 0)
            def _():
                wait_for(piece, scatter_recv)

            lax.fori_loop(1, CHIPS, pass_on, 0)

        steps = [SINGLE + 2 * j, SINGLE + 2 * j + 1]
        for i in steps:
            wait_for(qv.at[i], load_q.at[i])
        own_step(steps, qv, kcat, vcat, part)
        return carry

    lax.fori_loop(0, (FIRST - SINGLE) // 2, pair, 0)

    wait_for(gotkv.at[0], recv0kv)
    held = gotkv[...].astype(F32)
    kown[...] = jnp.concatenate([held[:, 8:], held[:, :8]], 1).astype(BF).reshape(32, D)
    vown[:, :D] = gotkv[...].reshape(32, D)
    vown[:, D:] = jnp.ones((32, D), BF)
    for copy in swaps:
        copy.wait_recv()

    def stretch(gl, carry):
        wait_for(got.at[gl, 0 : CHIPS - 1], recv1.at[gl])

        @pl.when(gl == 1)
        def _():
            give(0)

        stretch_step(gl, chip, core, got, kcat, vcat, kpeer, vpeer, kown, vown, sent, lse)
        return carry

    lax.fori_loop(0, 2, stretch, 0)

    @pl.when(ctx != 0)
    def _():
        wait_for(anc.at[0 : (CHIPS - 1) * PIECE], anc_recv)

    @pl.when(ctx != 1)
    def _():
        remote(half, half, core_send, core_recv, peer).start()

    for other in range(CHIPS):
        sent[other, 8] = level_tile(lse[0, other : other + 1, :] + lse[1, other : other + 1, :])

    give(1)

    parts[chip] = sent[chip]

    @pl.when(ctx != 0)
    def _():
        wait_for(half, core_recv)

    for g in range(GROUPS):
        kcat[g, :ANCHOR, :] = anc[g * ANCHOR : (g + 1) * ANCHOR, :]
        vcat[g, :ANCHOR, :D] = anc[(GROUPS + g) * ANCHOR : (GROUPS + g + 1) * ANCHOR, :]

    @pl.when(ctx == 0)
    def _():
        for g in range(GROUPS):
            key = kcat[g, ANCHOR : ANCHOR + 16, :].astype(F32)[0:1]
            kcat[g, :ANCHOR, :] = jnp.broadcast_to(key, (ANCHOR, D)).astype(BF)
            vcat[g, :ANCHOR, :] = jnp.zeros((ANCHOR, 2 * D), BF)

    rest = FIRST // 2
    hand = [
        pltpu.make_async_copy(kcat.at[pl.ds(rest, GROUPS - rest)], keys_out, put.at[FIRST]),
        pltpu.make_async_copy(vcat.at[pl.ds(rest, GROUPS - rest)], values_out, put.at[FIRST + 1]),
    ]
    for copy in hand:
        copy.start()

    def done(i, t):
        rows = pl.ds(t * TILE, TILE)
        pltpu.make_async_copy(qv.at[i, rows], out.at[i, rows], put.at[i]).start()

    def anchored(pair, carry):
        @pl.when(pair == MERGE)
        def _():
            wait_for(parts.at[0 : CHIPS - 1, 0:4], recv2.at[0])
            wait_for(parts.at[0 : CHIPS - 1, 4:9], recv2.at[1])
            merged = merge_step(parts).astype(BF).reshape(2, 4, 16, D)
            for gl in range(2):
                mine[:, gl] = merged[gl]
            for k in range(1, 4):
                other = (me + k) % 4
                remote(mine.at[other], last.at[me], send3, recv3, at_class(other)).start()
            last[me] = mine[me]

        anchor_step([1 + 2 * pair, 2 + 2 * pair], qv, kcat, vcat, part, done)
        return carry

    anchor_step([0], qv, kcat, vcat, part, done)
    lax.fori_loop(0, (FIRST - 1) // 2, anchored, 0)
    wait_for(last.at[0:3], recv3)
    result = pltpu.make_async_copy(last, stretch_out, put.at[FIRST + 2])
    result.start()

    for i in range(FIRST):
        pltpu.make_async_copy(qv.at[i], out.at[i], put.at[i]).wait()
    result.wait()
    for copy in hand:
        copy.wait()
    wait_for(cls.at[0:3], send0.at[0])
    wait_for(clskv.at[0], send0.at[1])
    for copy in swaps:
        copy.wait_send()
    for gl in range(2):
        wait_for(got.at[gl, 0 : CHIPS - 1], send1.at[gl])
    wait_for(sent.at[0 : CHIPS - 1, 0:4], send2.at[0])
    wait_for(sent.at[0 : CHIPS - 1, 4:9], send2.at[1])
    wait_for(mine.at[0:3], send3)

    @pl.when(ctx == 0)
    def _():
        wait_for(anc.at[0 : (2 * CHIPS - 1) * PIECE], scatter_send)

    @pl.when(ctx != 1)
    def _():
        wait_for(half, core_send)

    @pl.when((chip == 0) | (core == 1))
    def _():
        wait_for(anc.at[0 : (CHIPS - 1) * PIECE], anc_send)

    @pl.when((chip != 0) & (core == 0))
    def _():
        wait_for(anc.at[0 : (CHIPS - 2) * PIECE], anc_send)


def first_call(cq, ck, cv, sq, sk, sv):
    dma = pltpu.SemaphoreType.DMA
    vmem = pltpu.VMEM
    anywhere = pl.BlockSpec(memory_space=pl.ANY)
    rest = GROUPS - FIRST // 2
    return pl.pallas_call(
        first_kernel,
        in_specs=[anywhere] * 6,
        out_specs=[anywhere] * 4,
        out_shape=[
            jax.ShapeDtypeStruct((FIRST, ROWS, HS * D), BF),
            jax.ShapeDtypeStruct((rest, KEYS, D), BF),
            jax.ShapeDtypeStruct((rest, KEYS, 2 * D), BF),
            jax.ShapeDtypeStruct((4, 2, 16, D), BF),
        ],
        scratch_shapes=[
            vmem((2, 64 * D), BF),
            vmem((4, GROUPS * D), BF),
            vmem((4, GROUPS * D), BF),
            vmem((FIRST, ROWS, HS * D), BF),
            vmem((GROUPS, KEYS, D), BF),
            vmem((GROUPS, KEYS, 2 * D), BF),
            vmem((2, ROWS, D), BF),
            vmem((2, ROWS, 2 * D), BF),
            vmem((4, 2, 16, D), BF),
            vmem((2, 16, D), BF),
            vmem((2, CHIPS, 4, 16, D), BF),
            vmem((2, 16, D), BF),
            vmem((32, D), BF),
            vmem((32, 2 * D), BF),
            vmem((8 * ANCHOR, D), BF),
            vmem((FIRST, TILES, M, 2 * D), F32),
            vmem((CHIPS, 9, 16, D), BF),
            vmem((CHIPS, 9, 16, D), BF),
            vmem((2, CHIPS, D), F32),
            vmem((4, 2, 16, D), BF),
            vmem((4, 2, 16, D), BF),
            vmem((2, 16, D), F32),
            dma((3,)), dma((FIRST,)), dma((GROUPS,)), dma((GROUPS,)), dma((8,)), dma((FIRST + 3,)),
            dma((2,)), dma, dma, dma((4,)), dma((4,)), dma((2,)), dma((2,)),
            dma, dma, dma, dma, dma, dma,
            dma((2,)), dma((2,)), dma, dma,
        ],
        compiler_params=pltpu.CompilerParams(
            collective_id=0, has_side_effects=True, vmem_limit_bytes=58 * 2**20
        ),
        name="gather_stretch_first_heads",
    )(cq, ck, cv, sq, sk, sv)


def second_kernel(q, keys, values, last, before, out, stretch_out, ov, passing, rows_out, put, fetch, carry):
    i = pl.program_id(0)
    fetches = [pltpu.make_async_copy(before.at[j], passing.at[j], fetch.at[j]) for j in range(FIRST)]
    moves = [
        pltpu.make_async_copy(passing.at[j], out.at[:, j * HS * D : (j + 1) * HS * D], carry.at[j])
        for j in range(FIRST)
    ]
    result = pltpu.make_async_copy(rows_out, stretch_out, carry.at[FIRST])

    @pl.when(i == 0)
    def _():
        for copy in fetches:
            copy.start()
        for other in range(4):
            for gl in range(2):
                head = (other % 2) * 32 + (other // 2) * 16 + gl * 8
                held = last[other, gl].astype(F32)
                rows = [
                    jnp.concatenate([held[r * 8 + h : r * 8 + h + 1] for h in range(8)], 1) for r in range(2)
                ]
                rows_out[:, head * D : (head + 8) * D] = jnp.concatenate(rows, 0).astype(BF)
        result.start()

    def columns(step):
        return pl.ds(pl.multiple_of((FIRST + step) * HS * D, HS * D), HS * D)

    def done(t):
        rows = pl.ds(t * TILE, TILE)
        pltpu.make_async_copy(ov.at[i, rows], out.at[rows, columns(i)], put.at[i]).start()

    def between():
        @pl.when(i == 0)
        def _():
            for come, go in zip(fetches, moves):
                come.wait()
                go.start()

    @pl.when(lax.axis_index("ctx") >= 0)
    def _():
        whole_step(q, 0, ov, i, keys, values, 0, done, between)

    @pl.when(i == HALVES - FIRST - 1)
    def _():
        for step in range(HALVES - FIRST):
            pltpu.make_async_copy(ov.at[step], out.at[:, columns(step)], put.at[step]).wait()
        for copy in moves:
            copy.wait()
        result.wait()


def second_call(cq, keys, values, last, before):
    steps = HALVES - FIRST
    base = FIRST // 2

    def group(i):
        return (FIRST + i) // 2

    return pl.pallas_call(
        lambda q, *rest: second_kernel(OneStep(q), *rest),
        grid=(steps,),
        in_specs=[
            pl.BlockSpec((ROWS, HS * D), lambda i: (0, FIRST + i)),
            pl.BlockSpec((1, KEYS, D), lambda i: (group(i) - base, 0, 0)),
            pl.BlockSpec((1, KEYS, 2 * D), lambda i: (group(i) - base, 0, 0)),
            pl.BlockSpec((4, 2, 16, D), lambda i: (0, 0, 0, 0)),
            pl.BlockSpec(memory_space=pl.ANY),
        ],
        out_specs=[pl.BlockSpec(memory_space=pl.ANY), pl.BlockSpec(memory_space=pl.ANY)],
        out_shape=[
            jax.ShapeDtypeStruct((ROWS, 2 * GROUPS * HS * D), BF),
            jax.ShapeDtypeStruct((2, 64 * D), BF),
        ],
        scratch_shapes=[
            pltpu.VMEM((steps, ROWS, HS * D), BF),
            pltpu.VMEM((FIRST, ROWS, HS * D), BF),
            pltpu.VMEM((2, 64 * D), BF),
            pltpu.SemaphoreType.DMA((steps,)),
            pltpu.SemaphoreType.DMA((FIRST,)),
            pltpu.SemaphoreType.DMA((FIRST + 1,)),
        ],
        compiler_params=pltpu.CompilerParams(vmem_limit_bytes=58 * 2**20),
        name="last_heads",
    )(cq, keys, values, last, before)


class OneStep:
    def __init__(self, ref):
        self.ref = ref

    def __getitem__(self, index):
        return self.ref[index[1:]]


def body(cq, ck, cv, sq, sk, sv):
    before, keys, values, last = first_call(cq, ck, cv, sq, sk, sv)
    context_out, stretch_out = second_call(cq, keys, values, last, before)
    return context_out, stretch_out


def solution(mesh):
    in_specs = (
        P("ctx", "tp"),
        P("ctx", "tp"),
        P("ctx", "tp"),
        P(("ctx", "tp"), None),
        P("ctx", "tp"),
        P("ctx", "tp"),
    )
    out_specs = (P("ctx", "tp"), P(("ctx", "tp"), None))
    return jax.shard_map(body, mesh=mesh, in_specs=in_specs, out_specs=out_specs, check_vma=False)
```
